512 devices in a mesh: sec: 4 (over z_hi), fsdp: 128 (over z_lo, y, x, core).
Axes of the slice: x: 4, y: 8, z: 8 (z_hi: 4, z_lo: 2; z = z_hi * 2 + z_lo), core: 2. Of those that a mesh axis runs over, the one named last changes fastest.
Arguments:
- hidden: bfloat16 [65536, 4096], P('fsdp', 'sec'), may hold values from -24 to 24
- window_proj: bfloat16 [4, 4096, 512], P('sec', 'fsdp'), may hold values from -0.09375 to 0.09375
- head_weights: bfloat16 [4, 512], P('sec'), may hold values from -0.25 to 0.25
- ref_logprob: float32 [128, 512], P('fsdp'), may hold values from -4 to 0
- resp_spans: int32 [128, 2], P('fsdp'), may hold values from 64 to 512, as said below
Outputs:
- actor_grad: float32 [4, 4096, 256], P('sec', 'fsdp')
- advantage: float32 [128, 512], P('fsdp')
The draws below stay inside these ranges and needn't reach their ends.
Inputs may be any that keep to these rules, and one draw needn't show every extreme that they name: `resp_spans`: column 0 is a sequence's first response position, between 64 and 255; column 1 is one past its last response position, larger than column 0.
All inputs are finite; a program needn't handle non-finite values.
Results may differ from the reference program's by a relative error of at most 0.0085.
Values may be sent and summed in bfloat16 or wider, within the bound.
A program may use at most 64 MiB of HBM per device.

```python
import jax
import jax.numpy as jnp
from jax import lax

D = 4096
KW = 512
LEN = 512
SEQS = 128
TOKENS = 65536
N_SEC = 4


def draw_resp_spans(key, part):
    first_key, second_key = jax.random.split(key)
    starts = jax.random.randint(first_key, (SEQS, 1), LEN // 8, LEN // 2)
    rolled = jax.random.randint(second_key, (SEQS, 1), 0, 1 << 20)
    headroom = LEN - starts
    lengths = 1 + rolled % headroom
    return jnp.concatenate([starts, starts + lengths], axis=1).astype(jnp.int32)


def spiked(result, key, source, target, parts, factor):
    def block_of(dim):
        return (jnp.arange(result.shape[dim]) // (result.shape[dim] // parts)).reshape((-1,) + (1,) * (result.ndim - 1 - dim))

    first = jax.random.permutation(key, parts)[block_of(target)]
    second = (block_of(target) + parts // 2) % parts
    return jnp.where((block_of(source) == first) | (block_of(source) == second), factor * result, result)


def steps_of(key, shape, pieces, smallest, largest):
    def one(dim, parts):
        steps = jax.random.uniform(jax.random.fold_in(jax.random.fold_in(key, 6), dim), (parts,), jnp.float32, smallest / len(pieces), largest / len(pieces))
        return jnp.repeat(jnp.exp(steps), shape[dim] // parts).reshape((-1,) + (1,) * (len(shape) - dim - 1))

    level = one(*pieces[0])
    for cut in pieces[1:]:
        level = level * one(*cut)
    return level


def scatter_about(stream_key, extent, spread, limit, shards=(), kind=jnp.bfloat16):
    loudness = steps_of(stream_key, extent, shards, -0.22, 0.18) if shards else 1.0
    entries = jax.random.normal(stream_key, extent, jnp.float32) * spread * loudness
    return jnp.minimum(jnp.maximum(entries, -limit), limit).astype(kind)


def bell_draw_with(own_key, dims, deviation, most, cuts, heavy, dtype=jnp.bfloat16):
    array = deviation * jax.random.normal(own_key, dims, jnp.float32)
    if cuts:
        array = array * steps_of(own_key, dims, cuts, -0.22, 0.18)
    return jnp.clip(spiked(array, jax.random.fold_in(own_key, 3), *heavy), -most, most).astype(dtype)


def setup_inputs(seed: int = 0) -> dict:
    arg_keys = jax.random.split(jax.random.key(seed), 6)
    return {
        "hidden": bell_draw_with(arg_keys[0], (TOKENS, D), 1.0, 24.0, ((0, 128), (1, 4)), (0, 1, 128, 5.5)),
        "window_proj": scatter_about(arg_keys[1], (N_SEC, D, KW), D ** -0.5, 0.09375, ((0, 4), (1, 128))),
        "head_weights": scatter_about(arg_keys[2], (N_SEC, KW), KW ** -0.5, 0.25, ((0, 4),)),
        "ref_logprob": jnp.clip(-4.0 + 4.0 * jax.random.uniform(arg_keys[3], (SEQS, LEN), jnp.float32) ** steps_of(arg_keys[3], (SEQS, LEN), ((0, 128),), -0.2, 0.2), -4.0, 0.0),
        "resp_spans": draw_resp_spans(jax.random.fold_in(arg_keys[5], 71), 0),
    }


KL_COEF = 0.1
DISCOUNT = 1.0
TRACE_DECAY = 0.95
NORM_EPS = 1e-05

def silu_slope(values):
    sigmoid = jax.nn.sigmoid(values)
    return sigmoid * (1.0 + values * (1.0 - sigmoid))

def normalize(hidden):
    widened = hidden.astype(jnp.float32)
    meansq = lax.optimization_barrier(jnp.mean(widened * widened, axis=1, keepdims=True))
    return (widened * lax.rsqrt(meansq + NORM_EPS)).astype(jnp.bfloat16)

def advantage_of(log_prob, value_est, scores, ref_logprob, resp_spans, length):
    position = lax.broadcasted_iota(jnp.int32, (1, length), 1)
    starts = resp_spans[:, 0:1]
    ending = resp_spans[:, 1:2]
    inside = ((position >= starts) & (position < ending)).astype(jnp.float32)
    last_tok = (position == ending - 1).astype(jnp.float32)
    follow = (position + 1 < ending).astype(jnp.float32)
    reward = -KL_COEF * (log_prob - ref_logprob) * inside + scores * last_tok
    next_value = jnp.concatenate([value_est[:, 1:], jnp.zeros((value_est.shape[0], 1), jnp.float32)], axis=1)
    deltas = (reward + DISCOUNT * next_value * follow - value_est) * inside
    source_pos = lax.broadcasted_iota(jnp.int32, (length, length), 0)
    target_pos = lax.broadcasted_iota(jnp.int32, (length, length), 1)
    spacing = source_pos - target_pos
    decays = jnp.where(spacing >= 0, jnp.power(jnp.float32(DISCOUNT * TRACE_DECAY), jnp.maximum(spacing, 0).astype(jnp.float32)), jnp.float32(0.0))
    advantage = jnp.dot(deltas, decays, precision=lax.Precision.HIGHEST) * inside
    counts = (ending - starts).astype(jnp.float32)
    signal = -advantage / counts
    return (advantage, signal)

def reference(hidden, window_proj, head_weights, ref_logprob, resp_spans):
    normed = normalize(hidden)
    slabs = []
    head_sum = []
    for section in range(N_SEC):
        pre_act = jnp.dot(normed, window_proj[section], preferred_element_type=jnp.float32).astype(jnp.bfloat16)
        slabs.append(pre_act)
        head_sum.append(lax.optimization_barrier(jnp.sum(head_weights[section].astype(jnp.float32) * jax.nn.silu(pre_act.astype(jnp.float32)), axis=1)))
    log_prob = (head_sum[0] + head_sum[1]).reshape(SEQS, LEN)
    value_est = head_sum[2].reshape(SEQS, LEN)
    scores = head_sum[3].reshape(SEQS, LEN)
    advantage, signal = advantage_of(log_prob, value_est, scores, ref_logprob, resp_spans, LEN)
    flat_signal = signal.reshape(TOKENS)
    half_cols = KW // 2
    grads = []
    for quarter in range(N_SEC):
        section = quarter % 2
        offset = quarter // 2 * half_cols
        pre_part = slabs[section][:, offset:offset + half_cols].astype(jnp.float32)
        head_part = head_weights[section, offset:offset + half_cols].astype(jnp.float32)
        slopes = (flat_signal[:, None] * head_part[None, :] * silu_slope(pre_part)).astype(jnp.bfloat16)
        grads.append(lax.dot_general(normed, slopes, (((0,), (0,)), ((), ())), preferred_element_type=jnp.float32))
    return (jnp.stack(grads), advantage)
```

```python
import jax
import jax.numpy as jnp
from jax import lax
from jax.experimental import pallas as pl
from jax.experimental.pallas import tpu as pltpu
from jax.sharding import Mesh
from jax.sharding import PartitionSpec as P

AXES = ("h", "zl", "y", "x", "c")
FSDP = AXES[1:]
MESH = pl.DeviceIdType.MESH

NH, NZ, NY, NX, NC = 4, 2, 8, 4, 2
LEN = 512
SKIP = 64
TOK = (LEN - SKIP) // NH
SEQ = NZ * NC
ROWS = SEQ * TOK
FB = 1024
COLS = 128
D = NH * FB

KL_COEF = 0.1
DISCOUNT = 1.0
TRACE_DECAY = 0.95
NORM_EPS = 1e-05
HIGHEST = lax.Precision.HIGHEST

GROUP = [(a, b, e) for a in range(NH) for b in range(NZ) for e in range(NC) if (a, b, e) != (0, 0, 0)]


class Ids:
    def __init__(self):
        self.used = 0

    def take(self, count):
        first = self.used
        self.used += count
        return first


def plan():
    ids = Ids()
    out = {}
    for name in ("wg", "sd", "mg"):
        out[name] = ids.take(len(GROUP))
    out["hn"], out["hf"], out["hd"] = ids.take(3), ids.take(4), ids.take(8)
    for kind in ("ag", "rs"):
        for part in ("A", "B"):
            for axis, size in (("x", NX), ("y", NY)):
                for way in chains(size):
                    zl, sign, steps = way
                    out[kind, part, axis, zl, sign] = ids.take(steps)
    out["fn"] = ids.take(NH * NC)
    out["local"] = ids.take(2)
    out["total"] = ids.used
    return out


def chains(size):
    far, near = size // 2, size // 2 - 1
    return [(0, 1, far), (1, -1, far), (0, -1, near), (1, 1, near)]


PLAN = plan()


def kernel(
    hid, win, head, refl, spans, grad_out, adv_out,
    X, W, SIDE, MSG, SS, ACC, SL, G, ROWS4, STAGE, LAND, FIN, FR,
    ssem, rsem,
):
    h, zl, y, x, c = (lax.axis_index(a) for a in AXES)
    p = zl * NC + c
    pend = []

    def send(src, dst, sid, dev, rid=None):
        copy = pltpu.make_async_remote_copy(
            src_ref=src,
            dst_ref=dst,
            send_sem=ssem.at[sid],
            recv_sem=rsem.at[sid if rid is None else rid],
            device_id=dev,
            device_id_type=MESH,
        )
        copy.start()
        pend.append(copy)

    def arrived(ref, sid):
        pltpu.make_async_copy(ref, ref, rsem.at[sid]).wait()

    def peer(dh, dz, dc):
        return (lax.rem(h + dh, NH), lax.rem(zl + dz, NZ), y, x, lax.rem(c + dc, NC))

    def origin(dh, dz, dc):
        return (lax.rem(h + NH - dh, NH), lax.rem(zl + NZ - dz, NZ), lax.rem(c + NC - dc, NC))

    def place(axis, by):
        return lax.rem(x + 2 * NX + by, NX) if axis == "x" else lax.rem(y + 2 * NY + by, NY)

    def ring(axis, by):
        if axis == "x":
            return (h, zl, y, place("x", by), c)
        return (h, zl, place("y", by), x, c)

    barrier = pltpu.get_barrier_semaphore()
    mates = [peer(*o) for o in GROUP] + [ring("x", 1), ring("x", -1), ring("y", 1), ring("y", -1)]
    for dev in mates:
        pl.semaphore_signal(barrier, inc=1, device_id=dev, device_id_type=MESH)
    SIDE[h, p, 0:1, :] = refl[...]
    SIDE[h, p, 1:2, :] = jnp.full((1, LEN), spans[0, 0], jnp.int32).astype(jnp.float32)
    SIDE[h, p, 2:3, :] = jnp.full((1, LEN), spans[0, 1], jnp.int32).astype(jnp.float32)
    SIDE[h, p, 3:4, :] = head[...].astype(jnp.float32)
    SIDE[h, p, 4:8, :] = jnp.zeros((4, LEN), jnp.float32)
    MSG[h, p] = jnp.zeros((16, COLS), jnp.float32)
    SS[...] = jnp.zeros_like(SS)
    pl.semaphore_wait(barrier, len(mates))

    def wpiece(hs, zs, cs):
        return W.at[hs, zs * NY + y, x, pl.ds(pl.multiple_of(cs * 32, 32), 32), :]

    def wcols(zs, cs):
        return win.at[0, :, pl.ds(pl.multiple_of((zs * NC + cs) * COLS, COLS), COLS)]

    own_w = pltpu.make_async_copy(wcols(zl, c), wpiece(h, zl, c), rsem.at[PLAN["local"]])
    own_w.start()
    for n, off in enumerate(GROUP):
        dev = peer(*off)
        send(wcols(dev[1], dev[4]), wpiece(h, zl, c), PLAN["wg"] + n, dev)

    def unit(hd):
        return hid.at[pl.ds(pl.multiple_of(SKIP + hd * TOK, 16), TOK), :]

    partner = (h, 1 - zl, y, x, c)
    sibling = (h, zl, y, x, 1 - c)
    up, far, down = (lax.rem(h + by, NH) for by in (1, 2, 3))
    own_x = pltpu.make_async_copy(unit(h), X.at[h, p], rsem.at[PLAN["local"] + 1])
    own_x.start()
    send(unit(far), X.at[h, p], PLAN["hn"] + 2, (far, 1 - zl, y, x, c))
    send(unit(up), X.at[h, p], PLAN["hn"], (up, 0, y, x, c), PLAN["hn"] + zl)
    send(unit(down), X.at[h, p], PLAN["hn"] + 1, (down, 1, y, x, c), PLAN["hn"] + zl)
    send(unit(h), X.at[h, p], PLAN["hf"], partner)
    send(unit(h), X.at[h, p], PLAN["hd"], sibling)
    for n, off in enumerate(GROUP):
        send(SIDE.at[h, p], SIDE.at[h, p], PLAN["sd"] + n, peer(*off))

    def beside(z):
        return lax.rem(h + 3 + 2 * z, NH)

    def roles(z, core):
        first = [(h, z * NC + core), (beside(z), core), (beside(z), NC + core), (far, (1 - z) * NC + core)]
        other = 1 - z
        second = [(h, other * NC + core), (beside(other), core), (beside(other), NC + core), (far, z * NC + core)]
        return first, second

    firsts, seconds = roles(zl, c)
    theirs = sum(roles(zl, 1 - c), [])

    def squares(block, row):
        wide = X[block, row].astype(jnp.float32)
        wide = wide * wide
        part = wide[:, :COLS]
        for k in range(1, FB // COLS):
            part += wide[:, k * COLS : (k + 1) * COLS]
        SS[row] += part

    def first_arrived(n):
        block, row = firsts[n]
        ref = X.at[block, row]
        arrived(ref, PLAN["hn"] + n - 1)
        send(ref, ref, PLAN["hf"] + n, partner)
        send(ref, ref, PLAN["hd"] + n, sibling)
        squares(block, row)

    def second_arrived(n):
        block, row = seconds[n]
        ref = X.at[block, row]
        arrived(ref, PLAN["hf"] + n)
        send(ref, ref, PLAN["hd"] + 4 + n, sibling)
        squares(block, row)

    def third_arrived(n):
        block, row = theirs[n]
        arrived(X.at[block, row], PLAN["hd"] + n)
        squares(block, row)

    def piece(part, axis, half, pos):
        slabs = pl.ds(0 if part == "A" else 2, 2)
        if part == "A":
            if axis == "x":
                return W.at[slabs, half * NY + y, pos]
            return W.at[slabs, half * NY + pos]
        if axis == "y":
            return W.at[slabs, half * NY + pos, x]
        return W.at[slabs, pl.ds(half * NY, NY), pos]

    def gather_start(part, axis):
        for half, sign, _ in chains(NX if axis == "x" else NY):
            own = piece(part, axis, half, place(axis, 0))
            send(own, own, PLAN["ag", part, axis, half, sign], ring(axis, sign))

    def gather_step(part, axis, step):
        for half, sign, steps in chains(NX if axis == "x" else NY):
            if step > steps:
                continue
            base = PLAN["ag", part, axis, half, sign]
            got = piece(part, axis, half, place(axis, -sign * step))
            arrived(got, base + step - 1)
            if step < steps:
                send(got, got, base + step, ring(axis, sign))

    own_w.wait()
    for n, off in enumerate(GROUP):
        arrived(wpiece(*origin(*off)), PLAN["wg"] + n)
    gather_start("A", "x")
    gather_start("B", "y")
    gather_step("A", "x", 1)
    gather_step("B", "y", 1)
    gather_step("A", "x", 2)
    gather_start("A", "y")
    gather_step("B", "y", 2)
    gather_step("B", "y", 3)
    first_arrived(1)
    first_arrived(2)
    gather_step("B", "y", 4)
    gather_start("B", "x")
    gather_step("A", "y", 1)
    first_arrived(3)
    own_x.wait()
    squares(*firsts[0])
    gather_step("A", "y", 2)
    for n in range(3):
        second_arrived(n)
    gather_step("B", "x", 1)
    gather_step("A", "y", 3)
    second_arrived(3)
    for n in range(8):
        third_arrived(n)
    gather_step("B", "x", 2)
    gather_step("A", "y", 4)
    for n, off in enumerate(GROUP):
        hs, zs, cs = origin(*off)
        arrived(SIDE.at[hs, zs * NC + cs], PLAN["sd"] + n)

    ACC[...] = jnp.zeros_like(ACC)

    def project(j, carry):
        tokens = X[j].reshape(ROWS, FB)
        for k in range(2):
            sides = [W[2 * k + e, pl.ds(4 * j, 4)].reshape(FB, COLS) for e in range(2)]
            both = jnp.concatenate(sides, axis=1)
            product = jnp.dot(tokens, both, preferred_element_type=jnp.float32)
            ACC[:, :, 2 * COLS * k : 2 * COLS * (k + 1)] += product.reshape(SEQ, TOK, 2 * COLS)
        return carry

    lax.fori_loop(0, NH, project, 0)

    heads = [SIDE[s, p, 3:4, pl.ds(pl.multiple_of(p * COLS, COLS), COLS)] for s in range(4)]
    ones = jnp.ones((8, COLS), jnp.float32)

    def row_sums(values):
        sums = lax.dot_general(
            ones, values, (((1,), (1,)), ((), ())), precision=HIGHEST, preferred_element_type=jnp.float32
        )
        return sums[0:1, :]

    for i in range(SEQ):
        meansq = jnp.sum(SS[i], axis=1, keepdims=True) * (1.0 / D)
        scale = lax.rsqrt(meansq + NORM_EPS)
        weighted = []
        for s in range(4):
            raw = ACC[i, :, s * COLS : (s + 1) * COLS] * scale
            pre = raw.astype(jnp.bfloat16).astype(jnp.float32)
            sigmoid = 1.0 / (1.0 + jnp.exp(-pre))
            weighted.append(heads[s] * (pre * sigmoid))
            if s < 2:
                slope = sigmoid * (1.0 + pre * (1.0 - sigmoid))
                ACC[i, :, s * COLS : (s + 1) * COLS] = scale * heads[s] * slope
        MSG[h, p, i : i + 1, 0:TOK] = row_sums(weighted[0] + weighted[1])
        MSG[h, p, 4 + i : 5 + i, 0:TOK] = row_sums(weighted[2])
        MSG[h, p, 8 + i : 9 + i, 0:TOK] = row_sums(weighted[3])
    for n, off in enumerate(GROUP):
        send(MSG.at[h, p], MSG.at[h, p], PLAN["mg"] + n, peer(*off))

    for i in range(SEQ):
        for kind in range(3):
            ROWS4[kind, i : i + 1, :] = SIDE[h, i, kind : kind + 1, :]
    for n, off in enumerate(GROUP):
        hs, zs, cs = origin(*off)
        arrived(MSG.at[hs, zs * NC + cs], PLAN["mg"] + n)

    whole = jnp.zeros((16, LEN), jnp.float32)
    for a in range(NH):
        total = (MSG[a, 0] + MSG[a, 1]) + (MSG[a, 2] + MSG[a, 3])
        wide = jnp.concatenate([total, jnp.zeros((16, LEN - COLS), jnp.float32)], axis=1)
        whole += pltpu.roll(wide, SKIP + a * TOK, 1)
    log_prob, value_est, scores = whole[0:4], whole[4:8], whole[8:12]
    position = lax.broadcasted_iota(jnp.int32, (SEQ, LEN), 1)
    ref, starts, ending = ROWS4[0, 0:4, :], ROWS4[1, 0:4, :], ROWS4[2, 0:4, :]
    at = position.astype(jnp.float32)
    inside = jnp.where((at >= starts) & (at < ending), 1.0, 0.0)
    last_tok = jnp.where(at == ending - 1.0, 1.0, 0.0)
    follow = jnp.where(at + 1.0 < ending, 1.0, 0.0)
    reward = -KL_COEF * (log_prob - ref) * inside + scores * last_tok
    next_value = pltpu.roll(value_est, LEN - 1, 1)
    trail = (reward + DISCOUNT * next_value * follow - value_est) * inside
    span = 1
    while span < LEN:
        later = jnp.where(position + span < LEN, pltpu.roll(trail, LEN - span, 1), 0.0)
        trail += (DISCOUNT * TRACE_DECAY) ** span * later
        span *= 2
    advantage = trail * inside
    signal = -advantage / (ending - starts)
    mine = lax.broadcasted_iota(jnp.int32, (SEQ, LEN), 0) == p
    adv_out[...] = jnp.sum(jnp.where(mine, advantage, 0.0), axis=0, keepdims=True)

    near = jnp.zeros((SEQ, COLS), jnp.float32)
    for a in range(NH):
        turned = pltpu.roll(signal, LEN - SKIP - a * TOK, 1)[:, :COLS]
        near += jnp.where(h == a, turned, 0.0)
    square = jnp.concatenate([near, jnp.zeros((COLS - SEQ, COLS), jnp.float32)], axis=0).T
    for i in range(SEQ):
        factor = square[0:TOK, i : i + 1]
        SL[i] = (factor * ACC[i, :, 0 : 2 * COLS]).astype(jnp.bfloat16)

    def share(block, carry):
        j = lax.div(block, 4)
        lanes = pl.ds(pl.multiple_of(lax.rem(block, 4) * 256, 256), 256)
        tokens = X[j, :, :, lanes].reshape(ROWS, 256)
        product = lax.dot_general(
            tokens, SL[...].reshape(ROWS, 2 * COLS), (((0,), (0,)), ((), ())), preferred_element_type=jnp.float32
        )
        G[0, block] = product[:, :COLS].reshape(NX, 64, COLS)
        G[1, block] = product[:, COLS:].reshape(NX, 64, COLS)
        return carry

    lax.fori_loop(0, NZ * NY, share, 0)

    def at_of(part, axis, half, pos):
        if part == "A":
            return (0, half * NY + y, pos) if axis == "x" else (0, half * NY + pos)
        return (1, pl.ds(half * NY, NY), pos) if axis == "x" else (1, half * NY + pos, x)

    def room(buf, part, axis, sid):
        n = sid - PLAN["rs", part, axis, 0, 1]
        return buf[part, axis].at[n]

    def sum_send(part, axis, half, sign, steps, step):
        sid = PLAN["rs", part, axis, half, sign] + step - 1
        own = G[at_of(part, axis, half, place(axis, sign * (steps + 1 - step)))]
        if step > 1:
            own += room(LAND, part, axis, sid - 1)[...].astype(jnp.float32)
        stage = room(STAGE, part, axis, sid)
        stage[...] = own.astype(jnp.bfloat16)
        send(stage, room(LAND, part, axis, sid), sid, ring(axis, sign))

    def sum_step(part, axis, step):
        for half, sign, steps in chains(NX if axis == "x" else NY):
            if step > steps:
                continue
            if step > 0:
                sid = PLAN["rs", part, axis, half, sign] + step - 1
                arrived(room(LAND, part, axis, sid), sid)
                if step == steps:
                    mine_at = at_of(part, axis, half, place(axis, 0))
                    G[mine_at] = G[mine_at] + room(LAND, part, axis, sid)[...].astype(jnp.float32)
            if step < steps:
                sum_send(part, axis, half, sign, steps, step + 1)

    sum_step("A", "y", 0)
    sum_step("B", "x", 0)
    sum_step("A", "y", 1)
    sum_step("B", "x", 1)
    sum_step("A", "y", 2)
    sum_step("B", "x", 2)
    sum_step("B", "y", 0)
    sum_step("A", "y", 3)
    sum_step("B", "y", 1)
    sum_step("A", "y", 4)
    sum_step("A", "x", 0)
    sum_step("B", "y", 2)
    sum_step("A", "x", 1)
    sum_step("B", "y", 3)
    sum_step("A", "x", 2)
    sum_step("B", "y", 4)

    local = []
    for k in range(2):
        for half in range(NZ):
            FIN[k, half] = G[k, half * NY + y, x].astype(jnp.bfloat16)
            for core in range(NC):
                dest_h = k + 2 * zl
                src = FIN.at[k, half, pl.ds(core * 32, 32), :]
                dst = FR.at[h, c]
                rid = PLAN["fn"] + h * NC + c
                sid = PLAN["fn"] + (k * NZ + half) * NC + core
                here = (dest_h == h) & (half == zl) & (core == c)
                remote = pltpu.make_async_remote_copy(
                    src_ref=src,
                    dst_ref=dst,
                    send_sem=ssem.at[sid],
                    recv_sem=rsem.at[rid],
                    device_id=(dest_h, half, y, x, core),
                    device_id_type=MESH,
                )
                keep = pltpu.make_async_copy(src, dst, rsem.at[rid])
                pl.when(here)(keep.start)
                pl.when(jnp.logical_not(here))(remote.start)
                local.append((here, remote))
    for a in range(NH):
        for core in range(NC):
            arrived(FR.at[a, core], PLAN["fn"] + a * NC + core)
    for core in range(NC):
        parts = [FR[a, core].astype(jnp.float32) for a in range(NH)]
        grad_out[0, :, core * COLS : (core + 1) * COLS] = (parts[0] + parts[1]) + (parts[2] + parts[3])
    for here, remote in local:
        pl.when(jnp.logical_not(here))(remote.wait_send)
    for copy in pend:
        copy.wait_send()


def shards(hidden, window_proj, head_weights, ref_logprob, resp_spans):
    vmem = pl.BlockSpec(memory_space=pltpu.VMEM)
    hbm = pl.BlockSpec(memory_space=pl.ANY)
    bf16, f32 = jnp.bfloat16, jnp.float32
    rooms = {
        ("A", "y"): pltpu.VMEM((14, NX, 64, COLS), bf16),
        ("A", "x"): pltpu.VMEM((6, 64, COLS), bf16),
        ("B", "x"): pltpu.VMEM((6, NY, 64, COLS), bf16),
        ("B", "y"): pltpu.VMEM((14, 64, COLS), bf16),
    }
    return pl.pallas_call(
        kernel,
        out_shape=(
            jax.ShapeDtypeStruct((1, 32, 2 * COLS), f32),
            jax.ShapeDtypeStruct((1, LEN), f32),
        ),
        in_specs=[hbm, hbm, vmem, vmem, pl.BlockSpec(memory_space=pltpu.SMEM)],
        out_specs=(vmem, vmem),
        scratch_shapes=[
            pltpu.VMEM((NH, SEQ, TOK, FB), bf16),
            pltpu.VMEM((4, NZ * NY, NX, 64, COLS), bf16),
            pltpu.VMEM((NH, SEQ, 8, LEN), f32),
            pltpu.VMEM((NH, SEQ, 16, COLS), f32),
            pltpu.VMEM((SEQ, TOK, COLS), f32),
            pltpu.VMEM((SEQ, TOK, 4 * COLS), f32),
            pltpu.VMEM((SEQ, TOK, 2 * COLS), bf16),
            pltpu.VMEM((2, NZ * NY, NX, 64, COLS), f32),
            pltpu.VMEM((3, 8, LEN), f32),
            rooms,
            rooms,
            pltpu.VMEM((2, NZ, 64, COLS), bf16),
            pltpu.VMEM((NH, NC, 32, COLS), bf16),
            pltpu.SemaphoreType.DMA((PLAN["total"],)),
            pltpu.SemaphoreType.DMA((PLAN["total"],)),
        ],
        compiler_params=pltpu.CompilerParams(
            collective_id=0, has_side_effects=True, vmem_limit_bytes=48 * 1024 * 1024
        ),
    )(hidden, window_proj, head_weights, ref_logprob, resp_spans)


def solution(mesh):
    finer = Mesh(mesh.devices.reshape(NH, NZ, NY, NX, NC), AXES)
    return jax.shard_map(
        shards,
        mesh=finer,
        in_specs=(P(FSDP, "h"), P("h", FSDP, None), P("h", None), P(FSDP, None), P(FSDP, None)),
        out_specs=(P("h", FSDP, None), P(FSDP, None)),
        check_vma=False,
    )
```

```python
import jax
import jax.numpy as jnp
from jax import lax
from jax.experimental import pallas as pl
from jax.experimental.pallas import tpu as pltpu
from jax.sharding import Mesh
from jax.sharding import PartitionSpec as P

AXES = ("h", "zl", "y", "x", "c")
FSDP = AXES[1:]
MESH = pl.DeviceIdType.MESH

NH, NZ, NY, NX, NC = 4, 2, 8, 4, 2
LEN = 512
SKIP = 64
TOK = (LEN - SKIP) // NH
CUT = (48, 64)
SEQ = NZ * NC
ROWS = SEQ * TOK
FB = 1024
COLS = 128
D = NH * FB
NCHIP = NH * NZ

KL_COEF = 0.1
DISCOUNT = 1.0
TRACE_DECAY = 0.95
NORM_EPS = 1e-05
HIGHEST = lax.Precision.HIGHEST

GROUP = [(a, b, e) for a in range(NH) for b in range(NZ) for e in range(NC) if (a, b, e) != (0, 0, 0)]


def chains(size):
    far, near = size // 2, size // 2 - 1
    return [(0, 1, far), (1, -1, far), (0, -1, near), (1, 1, near)]


def plan():
    out = {}
    used = 0

    def take(name, count):
        nonlocal used
        out[name] = used
        used += count

    for name in ("wg", "sd", "mg"):
        take(name, len(GROUP))
    for odd in range(2):
        take(("hn", odd), 3)
        take(("hf", odd), 4)
        take(("hd", odd), 8)
    for kind, part, axis in (
        ("ag", "A", "x"),
        ("ag", "A", "y"),
        ("ag", "B", "y"),
        ("ag", "B", "x"),
        ("rs", "A", "y"),
        ("rs", "B", "x"),
    ):
        for half, sign, steps in chains(NX if axis == "x" else NY):
            take((kind, part, axis, half, sign), steps)
    take(("direct", "x"), NZ * (NX - 1))
    take(("direct", "y"), NZ * (NY - 1))
    take("fn", NH * NC)
    take("local", 8)
    out["total"] = used
    return out


PLAN = plan()


def kernel(
    hid, win, head_in, refl_in, spans_in, grad_out, adv_out,
    X, XT, W, SAY, SIDE, MSG, SS, ACC, SL, G, ROWS4, STAGE, LAND, FIN, FR, HEAD, REFL, SPANS,
    ssem, rsem,
):
    h, zl, y, x, c = (lax.axis_index(a) for a in AXES)
    p = zl * NC + c
    pend = []

    def send(src, dst, sid, dev, rid=None):
        copy = pltpu.make_async_remote_copy(
            src_ref=src,
            dst_ref=dst,
            send_sem=ssem.at[sid],
            recv_sem=rsem.at[sid if rid is None else rid],
            device_id=dev,
            device_id_type=MESH,
        )
        copy.start()
        pend.append(copy)

    def arrived(ref, sid):
        pltpu.make_async_copy(ref, ref, rsem.at[sid]).wait()

    def peer(dh, dz, dc):
        return (lax.rem(h + dh, NH), lax.rem(zl + dz, NZ), y, x, lax.rem(c + dc, NC))

    def origin(dh, dz, dc):
        return (lax.rem(h + NH - dh, NH), lax.rem(zl + NZ - dz, NZ), lax.rem(c + NC - dc, NC))

    def place(axis, by):
        return lax.rem(x + 2 * NX + by, NX) if axis == "x" else lax.rem(y + 2 * NY + by, NY)

    def ring(axis, by):
        if axis == "x":
            return (h, zl, y, place("x", by), c)
        return (h, zl, place("y", by), x, c)

    barrier = pltpu.get_barrier_semaphore()
    mates = [peer(*o) for o in GROUP]
    mates += [ring("x", by) for by in range(1, NX)] + [ring("y", by) for by in range(1, NY)]
    for dev in mates:
        pl.semaphore_signal(barrier, inc=1, device_id=dev, device_id_type=MESH)
    local = PLAN["local"]
    fetches = [
        pltpu.make_async_copy(src, dst, rsem.at[local + n])
        for n, (src, dst) in enumerate(((head_in, HEAD), (refl_in, REFL), (spans_in, SPANS)))
    ]
    for fetch in fetches:
        fetch.start()
    MSG[h, p] = jnp.zeros((8, COLS), jnp.float32)
    SS[...] = jnp.zeros_like(SS)
    SL[...] = jnp.zeros_like(SL)
    for fetch in fetches:
        fetch.wait()
    heads_wide = HEAD[...].astype(jnp.float32)
    for target in range(SEQ):
        for k in range(4):
            SAY[target, k : k + 1, :] = REFL[0:1, k * COLS : (k + 1) * COLS]
        for k in range(2):
            SAY[target, 4 + k : 5 + k, :] = jnp.full((1, COLS), SPANS[0, k], jnp.int32).astype(jnp.float32)
        SAY[target, 6:7, :] = heads_wide[:, target * COLS : (target + 1) * COLS]
        SAY[target, 7:8, :] = jnp.zeros((1, COLS), jnp.float32)
    SIDE[h, p] = SAY[p]
    pl.semaphore_wait(barrier, len(mates))

    def wpiece(hs, zs, cs):
        return W.at[hs, zs * NY + y, x, pl.ds(pl.multiple_of(cs * 32, 32), 32), :]

    def wcols(zs, cs):
        return win.at[0, :, pl.ds(pl.multiple_of((zs * NC + cs) * COLS, COLS), COLS)]

    own_w = pltpu.make_async_copy(wcols(zl, c), wpiece(h, zl, c), rsem.at[local + 3])
    own_w.start()
    for n, off in enumerate(GROUP):
        dev = peer(*off)
        send(wcols(dev[1], dev[4]), wpiece(h, zl, c), PLAN["wg"] + n, dev)

    chip = h * NZ + zl
    sibling = (h, zl, y, x, 1 - c)

    def seen(odd):
        turned = lax.rem(chip + NCHIP - odd, NCHIP)
        return lax.div(turned, NZ), lax.rem(turned, NZ)

    def real(odd, pair, side):
        turned = lax.rem(pair * NZ + side + odd, NCHIP)
        return lax.div(turned, NZ), lax.rem(turned, NZ)

    def rows_of(odd):
        return pl.ds(0, CUT[0]) if odd == 0 else pl.ds(CUT[0], CUT[1])

    def unit(odd, pair):
        start = SKIP + pair * TOK + (CUT[0] if odd else 0)
        return hid.at[pl.ds(pl.multiple_of(start, 16), CUT[odd]), :]

    def slot(odd, pair, side, core):
        block, low = real(odd, pair, side)
        return X.at[block, low * NC + core, rows_of(odd)]

    def roles(odd):
        pair, side = seen(odd)
        far = lax.rem(pair + 2, NH)

        def four(s):
            beside = lax.rem(pair + 3 + 2 * s, NH)
            return [(pair, s), (beside, 0), (beside, 1), (far, 1 - s)]

        return four(side), four(1 - side)

    own_x = []
    for odd in range(2):
        pair, side = seen(odd)
        up, far, down = (lax.rem(pair + by, NH) for by in (1, 2, 3))
        mine_at = slot(odd, pair, side, c)
        keep = pltpu.make_async_copy(unit(odd, pair), mine_at, rsem.at[local + 4 + odd])
        keep.start()
        own_x.append(keep)

        def to(dest, dest_side):
            block, low = real(odd, dest, dest_side)
            return (block, low, y, x, c)

        hn = PLAN["hn", odd]
        send(unit(odd, far), mine_at, hn + 2, to(far, 1 - side))
        send(unit(odd, up), mine_at, hn, to(up, 0), hn + side)
        send(unit(odd, down), mine_at, hn + 1, to(down, 1), hn + side)
        send(unit(odd, pair), mine_at, PLAN["hf", odd], to(pair, 1 - side))
        send(unit(odd, pair), mine_at, PLAN["hd", odd], sibling)
    for n, off in enumerate(GROUP):
        dev = peer(*off)
        send(SAY.at[dev[1] * NC + dev[4]], SIDE.at[h, p], PLAN["sd"] + n, dev)

    def firsts_arrived(odd):
        pair, side = seen(odd)
        block, low = real(odd, pair, 1 - side)
        for n in range(1, 4):
            ref = slot(odd, *roles(odd)[0][n], c)
            arrived(ref, PLAN["hn", odd] + n - 1)
            send(ref, ref, PLAN["hf", odd] + n, (block, low, y, x, c))
            send(ref, ref, PLAN["hd", odd] + n, sibling)

    def seconds_arrived(odd):
        for n in range(4):
            ref = slot(odd, *roles(odd)[1][n], c)
            arrived(ref, PLAN["hf", odd] + n)
            send(ref, ref, PLAN["hd", odd] + 4 + n, sibling)

    def settle(odd, which):
        if which == 0:
            own_x[odd].wait()
        for n in range(4):
            source = roles(odd)[which][n]
            arrived(slot(odd, *source, 1 - c), PLAN["hd", odd] + 4 * which + n)
            block, low = real(odd, *source)
            first = 0 if odd == 0 else CUT[0]
            both = X[block, pl.ds(low * NC, NC), first : first + CUT[odd], :]
            wide = both.astype(jnp.float32)
            wide = wide * wide
            part = wide[:, :, :COLS]
            for k in range(1, FB // COLS):
                part += wide[:, :, k * COLS : (k + 1) * COLS]
            SS[pl.ds(low * NC, NC), first : first + CUT[odd], :] += part
            flat = both.reshape(NC * CUT[odd], FB)
            if NC * CUT[odd] < COLS:
                flat = jnp.concatenate([flat, jnp.zeros((COLS - NC * CUT[odd], FB), jnp.bfloat16)], axis=0)
            lanes = pl.ds(pl.multiple_of((odd * NZ + low) * COLS, COLS), COLS)
            XT[block, :, lanes] = flat.T

    def piece(part, axis, half, pos):
        if part == "A":
            slabs = pl.ds(0, 2 - half)
        else:
            slabs = pl.ds(2 - half, 2 + half)
        if part == "A":
            if axis == "x":
                return W.at[slabs, half * NY + y, pos]
            return W.at[slabs, half * NY + pos]
        if axis == "y":
            return W.at[slabs, half * NY + pos, x]
        return W.at[slabs, pl.ds(half * NY, NY), pos]

    def gather_start(part, axis):
        for half, sign, _ in chains(NX if axis == "x" else NY):
            own = piece(part, axis, half, place(axis, 0))
            send(own, own, PLAN["ag", part, axis, half, sign], ring(axis, sign))

    def gather_step(part, axis, step):
        for half, sign, steps in chains(NX if axis == "x" else NY):
            if step > steps:
                continue
            base = PLAN["ag", part, axis, half, sign]
            got = piece(part, axis, half, place(axis, -sign * step))
            arrived(got, base + step - 1)
            if step < steps:
                send(got, got, base + step, ring(axis, sign))

    own_w.wait()
    for n, off in enumerate(GROUP):
        arrived(wpiece(*origin(*off)), PLAN["wg"] + n)
    gather_start("A", "x")
    gather_start("B", "y")
    gather_step("A", "x", 1)
    gather_step("B", "y", 1)
    gather_step("A", "x", 2)
    gather_start("A", "y")
    firsts_arrived(0)
    gather_step("B", "y", 2)
    gather_step("B", "y", 3)
    gather_step("B", "y", 4)
    gather_start("B", "x")
    settle(0, 0)
    seconds_arrived(0)
    gather_step("A", "y", 1)
    firsts_arrived(1)
    settle(0, 1)
    gather_step("A", "y", 2)
    gather_step("B", "x", 1)
    settle(1, 0)
    gather_step("A", "y", 3)
    seconds_arrived(1)
    settle(1, 1)
    gather_step("B", "x", 2)
    gather_step("A", "y", 4)
    for n, off in enumerate(GROUP):
        hs, zs, cs = origin(*off)
        arrived(SIDE.at[hs, zs * NC + cs], PLAN["sd"] + n)

    ACC[...] = jnp.zeros_like(ACC)

    def project(j, carry):
        tokens = X[j].reshape(ROWS, FB)
        for k in range(2):
            sides = [W[2 * k + e, pl.ds(4 * j, 4)].reshape(FB, COLS) for e in range(2)]
            both = jnp.concatenate(sides, axis=1)
            product = jnp.dot(tokens, both, preferred_element_type=jnp.float32)
            ACC[:, :, 2 * COLS * k : 2 * COLS * (k + 1)] += product.reshape(SEQ, TOK, 2 * COLS)
        return carry

    lax.fori_loop(0, NH, project, 0)

    heads = [SIDE[s, p, 6:7, :] for s in range(4)]
    ones = jnp.ones((8, COLS), jnp.float32)

    def row_sums(values):
        sums = lax.dot_general(
            ones, values, (((1,), (1,)), ((), ())), precision=HIGHEST, preferred_element_type=jnp.float32
        )
        return sums[0:1, :]

    lane = lax.broadcasted_iota(jnp.int32, (1, COLS), 1)
    blocks = (h, lax.rem(h + 3 + zl, NH))
    at_lane = (lane + SKIP + TOK * jnp.where(lane < CUT[0], blocks[0], blocks[1])).astype(jnp.float32)[:, :TOK]
    for i in range(SEQ):
        starts, ending = SIDE[h, i, 4:5, 0:TOK], SIDE[h, i, 5:6, 0:TOK]
        inside = jnp.where((at_lane >= starts) & (at_lane < ending), 1.0, 0.0)
        last_tok = jnp.where(at_lane == ending - 1.0, 1.0, 0.0)
        meansq = jnp.sum(SS[i], axis=1, keepdims=True) * (1.0 / D)
        scale = lax.rsqrt(meansq + NORM_EPS)
        weighted = []
        for s in range(4):
            raw = ACC[i, :, s * COLS : (s + 1) * COLS] * scale
            pre = raw.astype(jnp.bfloat16).astype(jnp.float32)
            sigmoid = 1.0 / (1.0 + jnp.exp(-pre))
            weighted.append(heads[s] * (pre * sigmoid))
            if s < 2:
                slope = sigmoid * (1.0 + pre * (1.0 - sigmoid))
                ACC[i, :, s * COLS : (s + 1) * COLS] = scale * heads[s] * slope
        log_prob = row_sums(weighted[0] + weighted[1])
        MSG[h, p, i : i + 1, 0:TOK] = -KL_COEF * log_prob * inside + row_sums(weighted[3]) * last_tok
        MSG[h, p, 4 + i : 5 + i, 0:TOK] = row_sums(weighted[2])
    for n, off in enumerate(GROUP):
        send(MSG.at[h, p], MSG.at[h, p], PLAN["mg"] + n, peer(*off))

    for i in range(SEQ):
        for k in range(4):
            part = slice(k * COLS, (k + 1) * COLS)
            ROWS4[0, i : i + 1, part] = SIDE[h, i, k : k + 1, :]
            ROWS4[1, i : i + 1, part] = SIDE[h, i, 4:5, :]
            ROWS4[2, i : i + 1, part] = SIDE[h, i, 5:6, :]
    for n, off in enumerate(GROUP):
        hs, zs, cs = origin(*off)
        arrived(MSG.at[hs, zs * NC + cs], PLAN["mg"] + n)

    whole = jnp.zeros((8, LEN), jnp.float32)
    for a in range(NH):
        nxt = (a + 1) % NH
        early = jnp.where(lane < CUT[0], MSG[a, 0] + MSG[a, 1], MSG[nxt, 0] + MSG[nxt, 1])
        total = early + (MSG[a, 2] + MSG[a, 3])
        wide = jnp.concatenate([total, jnp.zeros((8, LEN - COLS), jnp.float32)], axis=1)
        whole += pltpu.roll(wide, SKIP + a * TOK, 1)
    gains, value_est = whole[0:4], whole[4:8]
    position = lax.broadcasted_iota(jnp.int32, (SEQ, LEN), 1)
    ref, starts, ending = ROWS4[0, 0:4, :], ROWS4[1, 0:4, :], ROWS4[2, 0:4, :]
    at = position.astype(jnp.float32)
    inside = jnp.where((at >= starts) & (at < ending), 1.0, 0.0)
    follow = jnp.where(at + 1.0 < ending, 1.0, 0.0)
    reward = gains + KL_COEF * ref * inside
    next_value = pltpu.roll(value_est, LEN - 1, 1)
    trail = (reward + DISCOUNT * next_value * follow - value_est) * inside
    span = 1
    while span < LEN:
        later = jnp.where(position + span < LEN, pltpu.roll(trail, LEN - span, 1), 0.0)
        trail += (DISCOUNT * TRACE_DECAY) ** span * later
        span *= 2
    advantage = trail * inside
    signal = -advantage / (ending - starts)
    mine = lax.broadcasted_iota(jnp.int32, (SEQ, LEN), 0) == p
    adv_out[...] = jnp.sum(jnp.where(mine, advantage, 0.0), axis=0, keepdims=True)

    near = jnp.zeros((SEQ, COLS), jnp.float32)
    for a in range(NH):
        turned = pltpu.roll(signal, LEN - SKIP - a * TOK, 1)[:, :COLS]
        wanted = jnp.where(lane < CUT[0], blocks[0], blocks[1]) == a
        near += jnp.where(wanted, turned, 0.0)
    square = jnp.concatenate([near, jnp.zeros((COLS - SEQ, COLS), jnp.float32)], axis=0).T
    for i in range(SEQ):
        factor = square[0:TOK, i : i + 1]
        slopes = (factor * ACC[i, :, 0 : 2 * COLS]).astype(jnp.bfloat16)
        low, core = i // NC, i % NC
        for odd in range(2):
            first = (odd * NZ + low) * COLS + core * CUT[odd]
            taken = slice(0, CUT[0]) if odd == 0 else slice(CUT[0], TOK)
            SL[first : first + CUT[odd], :] = slopes[taken]

    def share(half, pos):
        block = half * NY + lax.rem(pos + 2 * NY, NY)
        j = lax.div(block, 4)
        features = pl.ds(pl.multiple_of(lax.rem(block, 4) * 256, 256), 256)
        product = jnp.dot(XT[j, features, :], SL[...], preferred_element_type=jnp.float32)
        G[0, block] = product[:, :COLS].reshape(NX, 64, COLS)
        G[1, block] = product[:, COLS:].reshape(NX, 64, COLS)

    def at_of(part, axis, half, pos):
        if part == "A":
            return (0, half * NY + y, pos) if axis == "x" else (0, half * NY + pos)
        return (1, pl.ds(half * NY, NY), pos) if axis == "x" else (1, half * NY + pos, x)

    def room(buf, part, axis, sid):
        return buf[part, axis].at[sid - PLAN["rs", part, axis, 0, 1]]

    def sum_send(part, axis, half, sign, steps, step):
        sid = PLAN["rs", part, axis, half, sign] + step - 1
        own = G[at_of(part, axis, half, place(axis, sign * (steps + 1 - step)))]
        if step > 1:
            own += room(LAND, part, axis, sid - 1)[...].astype(jnp.float32)
        stage = room(STAGE, part, axis, sid)
        stage[...] = own.astype(jnp.bfloat16)
        send(stage, room(LAND, part, axis, sid), sid, ring(axis, sign))

    def sum_step(part, axis, step):
        for half, sign, steps in chains(NX if axis == "x" else NY):
            if step > steps:
                continue
            sid = PLAN["rs", part, axis, half, sign] + step - 1
            arrived(room(LAND, part, axis, sid), sid)
            if step == steps:
                mine_at = at_of(part, axis, half, place(axis, 0))
                G[mine_at] = G[mine_at] + room(LAND, part, axis, sid)[...].astype(jnp.float32)
            else:
                sum_send(part, axis, half, sign, steps, step + 1)

    def direct_send(part, axis):
        size = NX if axis == "x" else NY
        for by in sorted(range(1, size), key=lambda d: -min(d, size - d)):
            for half in range(NZ):
                n = half * (size - 1) + by - 1
                stage = STAGE[part, axis].at[n]
                stage[...] = G[at_of(part, axis, half, place(axis, by))].astype(jnp.bfloat16)
                send(stage, LAND[part, axis].at[n], PLAN["direct", axis] + n, ring(axis, by))

    def direct_take(part, axis, k):
        size = NX if axis == "x" else NY
        for half in range(NZ):
            total = G[at_of(part, axis, half, place(axis, 0))]
            for by in range(1, size):
                n = half * (size - 1) + by - 1
                arrived(LAND[part, axis].at[n], PLAN["direct", axis] + n)
                total += LAND[part, axis][n].astype(jnp.float32)
            FIN[k, half] = total.astype(jnp.bfloat16)

    for half, sign, steps in chains(NY):
        share(half, y + sign * steps)
        sum_send("A", "y", half, sign, steps, 1)

    def shares(n, carry):
        share(0, y + 3 - n)
        share(1, y - 3 + n)
        return carry

    lax.fori_loop(0, NY - 2, shares, 0)
    for half, sign, steps in chains(NX):
        sum_send("B", "x", half, sign, steps, 1)
    sum_step("A", "y", 1)
    sum_step("B", "x", 1)
    sum_step("A", "y", 2)
    sum_step("B", "x", 2)
    direct_send("B", "y")
    sum_step("A", "y", 3)
    sum_step("A", "y", 4)
    direct_send("A", "x")

    handed = []
    for k, part, axis in ((1, "B", "y"), (0, "A", "x")):
        direct_take(part, axis, k)
        for half in range(NZ):
            for core in range(NC):
                dest_h = k + 2 * zl
                src = FIN.at[k, half, pl.ds(core * 32, 32), :]
                dst = FR.at[h, c]
                rid = PLAN["fn"] + h * NC + c
                sid = PLAN["fn"] + (k * NZ + half) * NC + core
                here = (dest_h == h) & (half == zl) & (core == c)
                remote = pltpu.make_async_remote_copy(
                    src_ref=src,
                    dst_ref=dst,
                    send_sem=ssem.at[sid],
                    recv_sem=rsem.at[rid],
                    device_id=(dest_h, half, y, x, core),
                    device_id_type=MESH,
                )
                keep = pltpu.make_async_copy(src, dst, rsem.at[rid])
                pl.when(here)(keep.start)
                pl.when(jnp.logical_not(here))(remote.start)
                handed.append((here, remote))
    for a in range(NH):
        for core in range(NC):
            arrived(FR.at[a, core], PLAN["fn"] + a * NC + core)
    for core in range(NC):
        parts = [FR[a, core].astype(jnp.float32) for a in range(NH)]
        grad_out[0, :, core * COLS : (core + 1) * COLS] = (parts[0] + parts[1]) + (parts[2] + parts[3])
    for here, remote in handed:
        pl.when(jnp.logical_not(here))(remote.wait_send)
    for copy in pend:
        copy.wait_send()


def shards(hidden, window_proj, head_weights, ref_logprob, resp_spans):
    vmem = pl.BlockSpec(memory_space=pltpu.VMEM)
    hbm = pl.BlockSpec(memory_space=pl.ANY)
    bf16, f32 = jnp.bfloat16, jnp.float32
    rooms = {
        ("A", "y"): pltpu.VMEM((14, NX, 64, COLS), bf16),
        ("A", "x"): pltpu.VMEM((6, 64, COLS), bf16),
        ("B", "x"): pltpu.VMEM((6, NY, 64, COLS), bf16),
        ("B", "y"): pltpu.VMEM((14, 64, COLS), bf16),
    }
    return pl.pallas_call(
        kernel,
        out_shape=(
            jax.ShapeDtypeStruct((1, 32, 2 * COLS), f32),
            jax.ShapeDtypeStruct((1, LEN), f32),
        ),
        in_specs=[hbm] * 5,
        out_specs=(vmem, vmem),
        scratch_shapes=[
            pltpu.VMEM((NH, SEQ, TOK, FB), bf16),
            pltpu.VMEM((NH, FB, 4 * COLS), bf16),
            pltpu.VMEM((4, NZ * NY, NX, 64, COLS), bf16),
            pltpu.VMEM((SEQ, 8, COLS), f32),
            pltpu.VMEM((NH, SEQ, 8, COLS), f32),
            pltpu.VMEM((NH, SEQ, 8, COLS), f32),
            pltpu.VMEM((SEQ, TOK, COLS), f32),
            pltpu.VMEM((SEQ, TOK, 4 * COLS), f32),
            pltpu.VMEM((4 * COLS, 2 * COLS), bf16),
            pltpu.VMEM((2, NZ * NY, NX, 64, COLS), f32),
            pltpu.VMEM((3, 8, LEN), f32),
            rooms,
            rooms,
            pltpu.VMEM((2, NZ, 64, COLS), bf16),
            pltpu.VMEM((NH, NC, 32, COLS), bf16),
            pltpu.VMEM((1, LEN), bf16),
            pltpu.VMEM((1, LEN), f32),
            pltpu.SMEM((1, 2), jnp.int32),
            pltpu.SemaphoreType.DMA((PLAN["total"],)),
            pltpu.SemaphoreType.DMA((PLAN["total"],)),
        ],
        compiler_params=pltpu.CompilerParams(
            collective_id=0, has_side_effects=True, vmem_limit_bytes=60 * 1024 * 1024
        ),
    )(hidden, window_proj, head_weights, ref_logprob, resp_spans)


def solution(mesh):
    finer = Mesh(mesh.devices.reshape(NH, NZ, NY, NX, NC), AXES)
    return jax.shard_map(
        shards,
        mesh=finer,
        in_specs=(P(FSDP, "h"), P("h", FSDP, None), P("h", None), P(FSDP, None), P(FSDP, None)),
        out_specs=(P("h", FSDP, None), P(FSDP, None)),
        check_vma=False,
    )
```

```python
import jax
import jax.numpy as jnp
from jax import lax
from jax.experimental import pallas as pl
from jax.experimental.pallas import tpu as pltpu
from jax.sharding import Mesh
from jax.sharding import PartitionSpec as P

AXES = ("h", "zl", "y", "x", "c")
FSDP = AXES[1:]
MESH = pl.DeviceIdType.MESH

NH, NZ, NY, NX, NC = 4, 2, 8, 4, 2
LEN = 512
SKIP = 64
TOK = (LEN - SKIP) // NH
CUT = (48, 64)
SEQ = NZ * NC
ROWS = SEQ * TOK
FB = 1024
COLS = 128
D = NH * FB
NCHIP = NH * NZ

KL_COEF = 0.1
DISCOUNT = 1.0
TRACE_DECAY = 0.95
NORM_EPS = 1e-05
HIGHEST = lax.Precision.HIGHEST

GROUP = [(a, b, e) for a in range(NH) for b in range(NZ) for e in range(NC) if (a, b, e) != (0, 0, 0)]


def chains(size):
    far, near = size // 2, size // 2 - 1
    return [(0, 1, far), (1, -1, far), (0, -1, near), (1, 1, near)]


def plan():
    out = {}
    used = 0

    def take(name, count):
        nonlocal used
        out[name] = used
        used += count

    for name in ("wg", "sd", "mg"):
        take(name, len(GROUP))
    for odd in range(2):
        for way in (1, -1):
            take(("hn", odd, way), 8)
        take(("hd", odd), 8)
    for part, axis in (("A", "x"), ("A", "y"), ("B", "y")):
        for half, sign, steps in chains(NX if axis == "x" else NY):
            take(("ag", part, axis, half, sign), steps)
    for half, sign, steps in chains(NX):
        take(("ag", "B", "x", half, sign), steps * NY)
    for part, axis in (("A", "y"), ("B", "x")):
        for sub in range(2):
            for half, sign, steps in chains(NX if axis == "x" else NY):
                take(("rs", part, axis, sub, half, sign), steps)
    take(("direct", "x"), NZ * (NX - 1))
    take(("direct", "y"), NZ * (NY - 1))
    take("fn", NH * NC)
    take("local", 8)
    out["total"] = used
    return out


PLAN = plan()


def kernel(
    hid, win, head_in, refl_in, spans_in, grad_out, adv_out,
    X, XT, W, SAY, SIDE, MSG, SS, ACC, SL, G, ROWS4, STAGE, LAND, FIN, FR, HEAD, REFL, SPANS,
    ssem, rsem,
):
    h, zl, y, x, c = (lax.axis_index(a) for a in AXES)
    p = zl * NC + c
    pend = []

    def send(src, dst, sid, dev, rid=None, when=None):
        copy = pltpu.make_async_remote_copy(
            src_ref=src,
            dst_ref=dst,
            send_sem=ssem.at[sid],
            recv_sem=rsem.at[sid if rid is None else rid],
            device_id=dev,
            device_id_type=MESH,
        )
        if when is None:
            copy.start()
        else:
            pl.when(when)(copy.start)
        pend.append((when, copy))

    def arrived(ref, sid, when=None):
        copy = pltpu.make_async_copy(ref, ref, rsem.at[sid])
        if when is None:
            copy.wait()
        else:
            pl.when(when)(copy.wait)

    def peer(dh, dz, dc):
        return (lax.rem(h + dh, NH), lax.rem(zl + dz, NZ), y, x, lax.rem(c + dc, NC))

    def origin(dh, dz, dc):
        return (lax.rem(h + NH - dh, NH), lax.rem(zl + NZ - dz, NZ), lax.rem(c + NC - dc, NC))

    def place(axis, by):
        return lax.rem(x + 2 * NX + by, NX) if axis == "x" else lax.rem(y + 2 * NY + by, NY)

    def ring(axis, by):
        if axis == "x":
            return (h, zl, y, place("x", by), c)
        return (h, zl, place("y", by), x, c)

    barrier = pltpu.get_barrier_semaphore()
    mates = [peer(*o) for o in GROUP]
    mates += [ring("x", by) for by in range(1, NX)] + [ring("y", by) for by in range(1, NY)]
    for dev in mates:
        pl.semaphore_signal(barrier, inc=1, device_id=dev, device_id_type=MESH)
    local = PLAN["local"]
    fetches = [
        pltpu.make_async_copy(src, dst, rsem.at[local + n])
        for n, (src, dst) in enumerate(((head_in, HEAD), (refl_in, REFL), (spans_in, SPANS)))
    ]
    for fetch in fetches:
        fetch.start()
    pl.semaphore_wait(barrier, len(mates))

    def wpiece(hs, zs, cs):
        return W.at[hs, zs * NY + y, x, pl.ds(pl.multiple_of(cs * 32, 32), 32), :]

    def wcols(zs, cs):
        return win.at[0, :, pl.ds(pl.multiple_of((zs * NC + cs) * COLS, COLS), COLS)]

    own_w = pltpu.make_async_copy(wcols(zl, c), wpiece(h, zl, c), rsem.at[local + 3])
    own_w.start()
    for n, off in enumerate(GROUP):
        dev = peer(*off)
        send(wcols(dev[1], dev[4]), wpiece(h, zl, c), PLAN["wg"] + n, dev)

    chip = h * NZ + zl
    sibling = (h, zl, y, x, 1 - c)

    def turn(by):
        return lax.rem(chip + 2 * NCHIP + by, NCHIP)

    def next_chip(way):
        to = turn(way)
        return (lax.div(to, NZ), lax.rem(to, NZ), y, x, c)

    def rows_of(odd):
        return pl.ds(0, CUT[0]) if odd == 0 else pl.ds(CUT[0], CUT[1])

    def unit(odd, pair):
        start = SKIP + pair * TOK + (CUT[0] if odd else 0)
        return hid.at[pl.ds(pl.multiple_of(start, 16), CUT[odd]), :]

    def kept(odd, origin, core):
        return X.at[origin * NC + core, rows_of(odd)]

    def passing(odd, way, n):
        return X.at[NCHIP * NC + (0 if way == 1 else 2) + n, rows_of(odd)]

    def side_of(odd, way):
        side = lax.rem(chip + odd, NZ)
        return side if way == 1 else 1 - side

    def hid_sem(odd, way, step, high):
        return PLAN["hn", odd, way] + 2 * (step - 1) + high

    def own_pair(odd):
        return lax.div(turn(-odd), NZ)

    def far_unit(odd, way, high):
        side = side_of(odd, way)
        if way == 1:
            return unit(odd, lax.div(turn(side + 2 * high - odd), NZ))
        return unit(odd, lax.div(turn(-1 - side - 2 * high - odd), NZ))

    def hid_send(odd, way, step, high):
        side = side_of(odd, way)
        origin = turn(-way * (step - 1))
        at_next = kept(odd, origin, c)
        when = None
        if step == 1:
            src = far_unit(odd, way, high)
            dst = passing(odd, way, 0) if high else at_next
        elif step == 2:
            src = passing(odd, way, 0) if high else kept(odd, origin, c)
            dst = at_next
            if high:
                dst = X.at[
                    jnp.where(side == 0, NCHIP * NC + (0 if way == 1 else 2) + 1, origin * NC + c), rows_of(odd)
                ]
            else:
                when = side == 0
        elif step == 3:
            src = X.at[jnp.where(side == 1, NCHIP * NC + (0 if way == 1 else 2) + 1, origin * NC + c), rows_of(odd)]
            dst = at_next
        else:
            src, dst, when = kept(odd, origin, c), at_next, side == 0
        send(src, dst, hid_sem(odd, way, step, high), next_chip(way), when=when)

    def share_unit(odd, n, origin):
        ref = kept(odd, origin, c)
        send(ref, ref, PLAN["hd", odd] + n, sibling)

    ORIGINS = (0, -1, 1, -2, 2, -3, 3, 4)

    def hid_take(odd, way, step, high):
        side = side_of(odd, way)
        origin = turn(-way * step)
        sem = hid_sem(odd, way, step, high)
        n = ORIGINS.index(-way * step) if step < 4 else 7
        ref = kept(odd, origin, c)
        if step == 1 and high:
            arrived(passing(odd, way, 0), sem)
            hid_send(odd, way, 2, 1)
        elif step == 1:
            arrived(ref, sem)
            hid_send(odd, way, 2, 0)
            share_unit(odd, n, origin)
        elif step == 2 and high:
            arrived(ref, sem)
            hid_send(odd, way, 3, 1)
        elif step == 2:
            arrived(ref, sem, side == 1)
            share_unit(odd, n, origin)
        elif step == 3:
            arrived(ref, sem)
            hid_send(odd, way, 4, 1)
            share_unit(odd, n, origin)
        else:
            arrived(ref, sem, side == 1)

    def takes(step, high):
        for odd in (1, 0):
            for way in (1, -1):
                hid_take(odd, way, step, high)
        if step == 4:
            for odd in (1, 0):
                share_unit(odd, 7, turn(4))

    own_x = []
    for odd in range(2):
        keep = pltpu.make_async_copy(unit(odd, own_pair(odd)), kept(odd, chip, c), rsem.at[local + 4 + odd])
        keep.start()
        own_x.append(keep)
    for high in (1, 0):
        for odd in (1, 0):
            for way in (1, -1):
                hid_send(odd, way, 1, high)
    for odd in range(2):
        send(unit(odd, own_pair(odd)), kept(odd, chip, c), PLAN["hd", odd], sibling)

    MSG[h, p] = jnp.zeros((8, COLS), jnp.float32)
    SS[...] = jnp.zeros_like(SS)
    SL[...] = jnp.zeros_like(SL)
    for fetch in fetches:
        fetch.wait()
    heads_wide = HEAD[...].astype(jnp.float32)
    for target in range(SEQ):
        for k in range(4):
            SAY[target, k : k + 1, :] = REFL[0:1, k * COLS : (k + 1) * COLS]
        for k in range(2):
            SAY[target, 4 + k : 5 + k, :] = jnp.full((1, COLS), SPANS[0, k], jnp.int32).astype(jnp.float32)
        SAY[target, 6:7, :] = heads_wide[:, target * COLS : (target + 1) * COLS]
        SAY[target, 7:8, :] = jnp.zeros((1, COLS), jnp.float32)
    SIDE[h, p] = SAY[p]
    for n, off in enumerate(GROUP):
        dev = peer(*off)
        send(SAY.at[dev[1] * NC + dev[4]], SIDE.at[h, p], PLAN["sd"] + n, dev)

    def settle(odd, which):
        for n in which:
            if n == 0:
                own_x[odd].wait()
            origin = turn(ORIGINS[n])
            block, low = lax.div(origin, NZ), lax.rem(origin, NZ)
            arrived(kept(odd, origin, 1 - c), PLAN["hd", odd] + n)
            first = 0 if odd == 0 else CUT[0]
            both = X[pl.ds(origin * NC, NC), first : first + CUT[odd], :]
            wide = both.astype(jnp.float32)
            wide = wide * wide
            part = wide[:, :, :COLS]
            for k in range(1, FB // COLS):
                part += wide[:, :, k * COLS : (k + 1) * COLS]
            SS[pl.ds(low * NC, NC), first : first + CUT[odd], :] += part
            flat = both.reshape(NC * CUT[odd], FB)
            if NC * CUT[odd] < COLS:
                flat = jnp.concatenate([flat, jnp.zeros((COLS - NC * CUT[odd], FB), jnp.bfloat16)], axis=0)
            lanes = pl.ds(pl.multiple_of((odd * NZ + low) * COLS, COLS), COLS)
            XT[block, :, lanes] = flat.T

    def piece(part, axis, half, pos):
        if part == "A":
            slabs = pl.ds(0, 2 - half)
        else:
            slabs = pl.ds(2 - half, 2 + half)
        if part == "A":
            if axis == "x":
                return W.at[slabs, half * NY + y, pos]
            return W.at[slabs, half * NY + pos]
        if axis == "y":
            return W.at[slabs, half * NY + pos, x]
        return W.at[slabs, pl.ds(half * NY, NY), pos]

    def gather_start(part, axis):
        for half, sign, _ in chains(NX if axis == "x" else NY):
            own = piece(part, axis, half, place(axis, 0))
            send(own, own, PLAN["ag", part, axis, half, sign], ring(axis, sign))

    def gather_step(part, axis, step):
        for half, sign, steps in chains(NX if axis == "x" else NY):
            if step > steps:
                continue
            base = PLAN["ag", part, axis, half, sign]
            got = piece(part, axis, half, place(axis, -sign * step))
            arrived(got, base + step - 1)
            if step < steps:
                send(got, got, base + step, ring(axis, sign))
            if part == "B":
                across_start(half, (-sign * step) % NY)

    def cell(half, by, pos):
        return W.at[pl.ds(2 - half, 2 + half), half * NY + place("y", by), pos]

    def across_start(half, by):
        for other, sign, steps in chains(NX):
            if other == half:
                own = cell(half, by, x)
                send(own, own, PLAN["ag", "B", "x", half, sign] + by * steps, ring("x", sign))

    def across_step(by, step):
        for half, sign, steps in chains(NX):
            if step > steps:
                continue
            base = PLAN["ag", "B", "x", half, sign] + by * steps
            got = cell(half, by, place("x", -sign * step))
            arrived(got, base + step - 1)
            if step < steps:
                send(got, got, base + step, ring("x", sign))

    own_w.wait()
    for n, off in enumerate(GROUP):
        arrived(wpiece(*origin(*off)), PLAN["wg"] + n)
    gather_start("A", "x")
    gather_start("B", "y")
    for half in range(NZ):
        across_start(half, 0)
    takes(1, 1)
    gather_step("A", "x", 1)
    gather_step("B", "y", 1)
    gather_step("A", "x", 2)
    gather_start("A", "y")
    across_step(0, 1)
    gather_step("B", "y", 2)
    takes(1, 0)
    across_step(1, 1)
    across_step(7, 1)
    gather_step("B", "y", 3)
    takes(2, 1)
    across_step(0, 2)
    across_step(2, 1)
    across_step(6, 1)
    gather_step("B", "y", 4)
    gather_step("A", "y", 1)
    takes(2, 0)
    for odd in range(2):
        settle(odd, (0, 1, 2))
    across_step(1, 2)
    across_step(7, 2)
    across_step(3, 1)
    across_step(5, 1)
    gather_step("A", "y", 2)
    takes(3, 1)
    across_step(2, 2)
    across_step(6, 2)
    across_step(4, 1)
    for odd in range(2):
        settle(odd, (3, 4))
    gather_step("A", "y", 3)
    across_step(3, 2)
    across_step(5, 2)
    takes(4, 1)
    across_step(4, 2)
    gather_step("A", "y", 4)
    for odd in range(2):
        settle(odd, (5, 6, 7))
    for n, off in enumerate(GROUP):
        hs, zs, cs = origin(*off)
        arrived(SIDE.at[hs, zs * NC + cs], PLAN["sd"] + n)

    ACC[...] = jnp.zeros_like(ACC)

    def project(j, carry):
        tokens = X[pl.ds(4 * j, 4)].reshape(ROWS, FB)
        for k in range(2):
            sides = [W[2 * k + e, pl.ds(4 * j, 4)].reshape(FB, COLS) for e in range(2)]
            both = jnp.concatenate(sides, axis=1)
            product = jnp.dot(tokens, both, preferred_element_type=jnp.float32)
            ACC[:, :, 2 * COLS * k : 2 * COLS * (k + 1)] += product.reshape(SEQ, TOK, 2 * COLS)
        return carry

    lax.fori_loop(0, NH, project, 0)

    heads = [SIDE[s, p, 6:7, :] for s in range(4)]
    ones = jnp.ones((8, COLS), jnp.float32)

    def row_sums(values):
        sums = lax.dot_general(
            ones, values, (((1,), (1,)), ((), ())), precision=HIGHEST, preferred_element_type=jnp.float32
        )
        return sums[0:1, :]

    lane = lax.broadcasted_iota(jnp.int32, (1, COLS), 1)
    blocks = (h, lax.rem(h + 3 + zl, NH))
    at_lane = (lane + SKIP + TOK * jnp.where(lane < CUT[0], blocks[0], blocks[1])).astype(jnp.float32)[:, :TOK]
    for i in range(SEQ):
        starts, ending = SIDE[h, i, 4:5, 0:TOK], SIDE[h, i, 5:6, 0:TOK]
        inside = jnp.where((at_lane >= starts) & (at_lane < ending), 1.0, 0.0)
        last_tok = jnp.where(at_lane == ending - 1.0, 1.0, 0.0)
        meansq = jnp.sum(SS[i], axis=1, keepdims=True) * (1.0 / D)
        scale = lax.rsqrt(meansq + NORM_EPS)
        weighted = []
        for s in range(4):
            raw = ACC[i, :, s * COLS : (s + 1) * COLS] * scale
            pre = raw.astype(jnp.bfloat16).astype(jnp.float32)
            sigmoid = 1.0 / (1.0 + jnp.exp(-pre))
            weighted.append(heads[s] * (pre * sigmoid))
            if s < 2:
                slope = sigmoid * (1.0 + pre * (1.0 - sigmoid))
                ACC[i, :, s * COLS : (s + 1) * COLS] = scale * heads[s] * slope
        log_prob = row_sums(weighted[0] + weighted[1])
        MSG[h, p, i : i + 1, 0:TOK] = -KL_COEF * log_prob * inside + row_sums(weighted[3]) * last_tok
        MSG[h, p, 4 + i : 5 + i, 0:TOK] = row_sums(weighted[2])
    for n, off in enumerate(GROUP):
        send(MSG.at[h, p], MSG.at[h, p], PLAN["mg"] + n, peer(*off))

    for i in range(SEQ):
        for k in range(4):
            part = slice(k * COLS, (k + 1) * COLS)
            ROWS4[0, i : i + 1, part] = SIDE[h, i, k : k + 1, :]
            ROWS4[1, i : i + 1, part] = SIDE[h, i, 4:5, :]
            ROWS4[2, i : i + 1, part] = SIDE[h, i, 5:6, :]
    for n, off in enumerate(GROUP):
        hs, zs, cs = origin(*off)
        arrived(MSG.at[hs, zs * NC + cs], PLAN["mg"] + n)

    whole = jnp.zeros((8, LEN), jnp.float32)
    for a in range(NH):
        nxt = (a + 1) % NH
        early = jnp.where(lane < CUT[0], MSG[a, 0] + MSG[a, 1], MSG[nxt, 0] + MSG[nxt, 1])
        total = early + (MSG[a, 2] + MSG[a, 3])
        wide = jnp.concatenate([total, jnp.zeros((8, LEN - COLS), jnp.float32)], axis=1)
        whole += pltpu.roll(wide, SKIP + a * TOK, 1)
    gains, value_est = whole[0:4], whole[4:8]
    position = lax.broadcasted_iota(jnp.int32, (SEQ, LEN), 1)
    ref, starts, ending = ROWS4[0, 0:4, :], ROWS4[1, 0:4, :], ROWS4[2, 0:4, :]
    at = position.astype(jnp.float32)
    inside = jnp.where((at >= starts) & (at < ending), 1.0, 0.0)
    follow = jnp.where(at + 1.0 < ending, 1.0, 0.0)
    reward = gains + KL_COEF * ref * inside
    next_value = pltpu.roll(value_est, LEN - 1, 1)
    trail = (reward + DISCOUNT * next_value * follow - value_est) * inside
    span = 1
    while span < LEN:
        later = jnp.where(position + span < LEN, pltpu.roll(trail, LEN - span, 1), 0.0)
        trail += (DISCOUNT * TRACE_DECAY) ** span * later
        span *= 2
    advantage = trail * inside
    signal = -advantage / (ending - starts)
    mine = lax.broadcasted_iota(jnp.int32, (SEQ, LEN), 0) == p
    adv_out[...] = jnp.sum(jnp.where(mine, advantage, 0.0), axis=0, keepdims=True)

    near = jnp.zeros((SEQ, COLS), jnp.float32)
    for a in range(NH):
        turned = pltpu.roll(signal, LEN - SKIP - a * TOK, 1)[:, :COLS]
        wanted = jnp.where(lane < CUT[0], blocks[0], blocks[1]) == a
        near += jnp.where(wanted, turned, 0.0)
    square = jnp.concatenate([near, jnp.zeros((COLS - SEQ, COLS), jnp.float32)], axis=0).T
    for i in range(SEQ):
        factor = square[0:TOK, i : i + 1]
        slopes = (factor * ACC[i, :, 0 : 2 * COLS]).astype(jnp.bfloat16)
        low, core = i // NC, i % NC
        for odd in range(2):
            first = (odd * NZ + low) * COLS + core * CUT[odd]
            taken = slice(0, CUT[0]) if odd == 0 else slice(CUT[0], TOK)
            SL[first : first + CUT[odd], :] = slopes[taken]

    def share(half, pos):
        block = half * NY + lax.rem(pos + 2 * NY, NY)
        j = lax.div(block, 4)
        features = pl.ds(pl.multiple_of(lax.rem(block, 4) * 256, 256), 256)
        product = jnp.dot(XT[j, features, :], SL[...], preferred_element_type=jnp.float32)
        G[0, block] = product[:, :COLS].reshape(NX, 64, COLS)
        G[1, block] = product[:, COLS:].reshape(NX, 64, COLS)

    def at_of(part, axis, half, pos, sub=None):
        if part == "A":
            if axis == "x":
                return (0, half * NY + y, pos)
            return (0, half * NY + pos, pl.ds(2 * sub, 2))
        if axis == "x":
            return (1, pl.ds(half * NY + 4 * sub, 4), pos)
        return (1, half * NY + pos, x)

    def room(buf, part, axis, sid):
        return buf[part, axis].at[sid - PLAN["rs", part, axis, 0, 0, 1]]

    def sum_send(part, axis, sub, half, sign, steps, step):
        sid = PLAN["rs", part, axis, sub, half, sign] + step - 1
        own = G[at_of(part, axis, half, place(axis, sign * (steps + 1 - step)), sub)]
        if step > 1:
            own += room(LAND, part, axis, sid - 1)[...].astype(jnp.float32)
        stage = room(STAGE, part, axis, sid)
        stage[...] = own.astype(jnp.bfloat16)
        send(stage, room(LAND, part, axis, sid), sid, ring(axis, sign))

    def sum_step(part, axis, step, sub):
        for half, sign, steps in chains(NX if axis == "x" else NY):
            if step > steps:
                continue
            sid = PLAN["rs", part, axis, sub, half, sign] + step - 1
            arrived(room(LAND, part, axis, sid), sid)
            if step == steps:
                mine_at = at_of(part, axis, half, place(axis, 0), sub)
                G[mine_at] = G[mine_at] + room(LAND, part, axis, sid)[...].astype(jnp.float32)
            else:
                sum_send(part, axis, sub, half, sign, steps, step + 1)

    def direct_send(part, axis):
        size = NX if axis == "x" else NY
        for by in sorted(range(1, size), key=lambda d: -min(d, size - d)):
            for half in range(NZ):
                n = half * (size - 1) + by - 1
                stage = STAGE[part, axis].at[n]
                stage[...] = G[at_of(part, axis, half, place(axis, by))].astype(jnp.bfloat16)
                send(stage, LAND[part, axis].at[n], PLAN["direct", axis] + n, ring(axis, by))

    def direct_take(part, axis, k):
        size = NX if axis == "x" else NY
        for half in range(NZ):
            total = G[at_of(part, axis, half, place(axis, 0))]
            for by in range(1, size):
                n = half * (size - 1) + by - 1
                arrived(LAND[part, axis].at[n], PLAN["direct", axis] + n)
                total += LAND[part, axis][n].astype(jnp.float32)
            FIN[k, half] = total.astype(jnp.bfloat16)

    for half, sign, steps in chains(NY):
        share(half, y + sign * steps)
        sum_send("A", "y", 0, half, sign, steps, 1)
    for half, sign, steps in chains(NY):
        sum_send("A", "y", 1, half, sign, steps, 1)

    def shares(n, carry):
        share(0, y + 3 - n)
        share(1, y - 3 + n)
        return carry

    lax.fori_loop(0, NY - 2, shares, 0)
    for sub in range(2):
        for half, sign, steps in chains(NX):
            sum_send("B", "x", sub, half, sign, steps, 1)
    sum_step("A", "y", 1, 0)
    sum_step("A", "y", 1, 1)
    sum_step("B", "x", 1, 0)
    sum_step("B", "x", 1, 1)
    sum_step("A", "y", 2, 0)
    sum_step("A", "y", 2, 1)
    sum_step("B", "x", 2, 0)
    sum_step("B", "x", 2, 1)
    direct_send("B", "y")
    sum_step("A", "y", 3, 0)
    sum_step("A", "y", 3, 1)
    sum_step("A", "y", 4, 0)
    sum_step("A", "y", 4, 1)
    direct_send("A", "x")

    handed = []
    for k, part, axis in ((1, "B", "y"), (0, "A", "x")):
        direct_take(part, axis, k)
        for half in range(NZ):
            for core in range(NC):
                dest_h = k + 2 * zl
                src = FIN.at[k, half, pl.ds(core * 32, 32), :]
                dst = FR.at[h, c]
                rid = PLAN["fn"] + h * NC + c
                sid = PLAN["fn"] + (k * NZ + half) * NC + core
                here = (dest_h == h) & (half == zl) & (core == c)
                remote = pltpu.make_async_remote_copy(
                    src_ref=src,
                    dst_ref=dst,
                    send_sem=ssem.at[sid],
                    recv_sem=rsem.at[rid],
                    device_id=(dest_h, half, y, x, core),
                    device_id_type=MESH,
                )
                keep = pltpu.make_async_copy(src, dst, rsem.at[rid])
                pl.when(here)(keep.start)
                pl.when(jnp.logical_not(here))(remote.start)
                handed.append((here, remote))
    for a in range(NH):
        for core in range(NC):
            arrived(FR.at[a, core], PLAN["fn"] + a * NC + core)
    for core in range(NC):
        parts = [FR[a, core].astype(jnp.float32) for a in range(NH)]
        grad_out[0, :, core * COLS : (core + 1) * COLS] = (parts[0] + parts[1]) + (parts[2] + parts[3])
    for here, remote in handed:
        pl.when(jnp.logical_not(here))(remote.wait_send)
    for when, copy in pend:
        if when is None:
            copy.wait_send()
        else:
            pl.when(when)(copy.wait_send)


def shards(hidden, window_proj, head_weights, ref_logprob, resp_spans):
    vmem = pl.BlockSpec(memory_space=pltpu.VMEM)
    hbm = pl.BlockSpec(memory_space=pl.ANY)
    bf16, f32 = jnp.bfloat16, jnp.float32
    rooms = {
        ("A", "y"): pltpu.VMEM((28, NX // 2, 64, COLS), bf16),
        ("A", "x"): pltpu.VMEM((6, 64, COLS), bf16),
        ("B", "x"): pltpu.VMEM((12, NY // 2, 64, COLS), bf16),
        ("B", "y"): pltpu.VMEM((14, 64, COLS), bf16),
    }
    return pl.pallas_call(
        kernel,
        out_shape=(
            jax.ShapeDtypeStruct((1, 32, 2 * COLS), f32),
            jax.ShapeDtypeStruct((1, LEN), f32),
        ),
        in_specs=[hbm] * 5,
        out_specs=(vmem, vmem),
        scratch_shapes=[
            pltpu.VMEM((NCHIP * NC + 4, TOK, FB), bf16),
            pltpu.VMEM((NH, FB, 4 * COLS), bf16),
            pltpu.VMEM((4, NZ * NY, NX, 64, COLS), bf16),
            pltpu.VMEM((SEQ, 8, COLS), f32),
            pltpu.VMEM((NH, SEQ, 8, COLS), f32),
            pltpu.VMEM((NH, SEQ, 8, COLS), f32),
            pltpu.VMEM((SEQ, TOK, COLS), f32),
            pltpu.VMEM((SEQ, TOK, 4 * COLS), f32),
            pltpu.VMEM((4 * COLS, 2 * COLS), bf16),
            pltpu.VMEM((2, NZ * NY, NX, 64, COLS), f32),
            pltpu.VMEM((3, 8, LEN), f32),
            rooms,
            rooms,
            pltpu.VMEM((2, NZ, 64, COLS), bf16),
            pltpu.VMEM((NH, NC, 32, COLS), bf16),
            pltpu.VMEM((1, LEN), bf16),
            pltpu.VMEM((1, LEN), f32),
            pltpu.SMEM((1, 2), jnp.int32),
            pltpu.SemaphoreType.DMA((PLAN["total"],)),
            pltpu.SemaphoreType.DMA((PLAN["total"],)),
        ],
        compiler_params=pltpu.CompilerParams(
            collective_id=0, has_side_effects=True, vmem_limit_bytes=60 * 1024 * 1024
        ),
    )(hidden, window_proj, head_weights, ref_logprob, resp_spans)


def solution(mesh):
    finer = Mesh(mesh.devices.reshape(NH, NZ, NY, NX, NC), AXES)
    return jax.shard_map(
        shards,
        mesh=finer,
        in_specs=(P(FSDP, "h"), P("h", FSDP, None), P("h", None), P(FSDP, None), P(FSDP, None)),
        out_specs=(P("h", FSDP, None), P(FSDP, None)),
        check_vma=False,
    )
```

```python
import jax
import jax.numpy as jnp
from jax import lax
from jax.experimental import pallas as pl
from jax.experimental.pallas import tpu as pltpu
from jax.sharding import Mesh
from jax.sharding import PartitionSpec as P

AXES = ("h", "zl", "y", "x", "c")
FSDP = AXES[1:]
MESH = pl.DeviceIdType.MESH

NH, NZ, NY, NX, NC = 4, 2, 8, 4, 2
LEN = 512
SKIP = 64
TOK = (LEN - SKIP) // NH
CUT = (48, 64)
SEQ = NZ * NC
ROWS = SEQ * TOK
FB = 1024
COLS = 128
D = NH * FB
NCHIP = NH * NZ

KL_COEF = 0.1
DISCOUNT = 1.0
TRACE_DECAY = 0.95
NORM_EPS = 1e-05
HIGHEST = lax.Precision.HIGHEST

GROUP = [(a, b, e) for a in (2, 1, 3, 0) for b in range(NZ) for e in range(NC) if (a, b, e) != (0, 0, 0)]


def chains(size):
    far, near = size // 2, size // 2 - 1
    return [(0, 1, far), (1, -1, far), (0, -1, near), (1, 1, near)]


def plan():
    out = {}
    used = 0

    def take(name, count):
        nonlocal used
        out[name] = used
        used += count

    for name in ("wg", "sd", "mg"):
        take(name, len(GROUP))
    for odd in range(2):
        for way in (1, -1):
            take(("hn", odd, way), 8)
        take(("hd", odd), 8)
    for part, axis in (("A", "x"), ("A", "y"), ("B", "y")):
        for half, sign, steps in chains(NX if axis == "x" else NY):
            take(("ag", part, axis, half, sign), steps)
    for half, sign, steps in chains(NX):
        take(("ag", "B", "x", half, sign), steps * NY)
    for part, axis in (("A", "y"), ("B", "x")):
        for sub in range(2):
            for half, sign, steps in chains(NX if axis == "x" else NY):
                take(("rs", part, axis, sub, half, sign), steps)
    take(("direct", "x"), NZ * (NX - 1))
    take(("direct", "y"), NZ * (NY - 1))
    take("fn", NH * NC)
    take("local", 8)
    out["total"] = used
    return out


PLAN = plan()


def kernel(
    hid, win, head_in, refl_in, spans_in, grad_out, adv_out,
    X, XT, W, SAY, SIDE, MSG, SS, ACC, SL, G, ROWS4, STAGE, LAND, FIN, FR, HEAD, REFL, SPANS,
    ssem, rsem,
):
    h, zl, y, x, c = (lax.axis_index(a) for a in AXES)
    p = zl * NC + c
    pend = []

    def send(src, dst, sid, dev, rid=None, when=None):
        copy = pltpu.make_async_remote_copy(
            src_ref=src,
            dst_ref=dst,
            send_sem=ssem.at[sid],
            recv_sem=rsem.at[sid if rid is None else rid],
            device_id=dev,
            device_id_type=MESH,
        )
        if when is None:
            copy.start()
        else:
            pl.when(when)(copy.start)
        pend.append((when, copy))

    def arrived(ref, sid, when=None):
        copy = pltpu.make_async_copy(ref, ref, rsem.at[sid])
        if when is None:
            copy.wait()
        else:
            pl.when(when)(copy.wait)

    def peer(dh, dz, dc):
        return (lax.rem(h + dh, NH), lax.rem(zl + dz, NZ), y, x, lax.rem(c + dc, NC))

    def origin(dh, dz, dc):
        return (lax.rem(h + NH - dh, NH), lax.rem(zl + NZ - dz, NZ), lax.rem(c + NC - dc, NC))

    def place(axis, by):
        return lax.rem(x + 2 * NX + by, NX) if axis == "x" else lax.rem(y + 2 * NY + by, NY)

    def ring(axis, by):
        if axis == "x":
            return (h, zl, y, place("x", by), c)
        return (h, zl, place("y", by), x, c)

    barrier = pltpu.get_barrier_semaphore()
    mates = [peer(*o) for o in GROUP]
    mates += [ring("x", by) for by in range(1, NX)] + [ring("y", by) for by in range(1, NY)]
    for dev in mates:
        pl.semaphore_signal(barrier, inc=1, device_id=dev, device_id_type=MESH)
    local = PLAN["local"]
    fetches = [
        pltpu.make_async_copy(src, dst, rsem.at[local + n])
        for n, (src, dst) in enumerate(((head_in, HEAD), (refl_in, REFL), (spans_in, SPANS)))
    ]
    for fetch in fetches:
        fetch.start()
    pl.semaphore_wait(barrier, len(mates))

    def wpiece(hs, zs, cs):
        return W.at[hs, zs * NY + y, x, pl.ds(pl.multiple_of(cs * 32, 32), 32), :]

    def wcols(zs, cs):
        return win.at[0, :, pl.ds(pl.multiple_of((zs * NC + cs) * COLS, COLS), COLS)]

    own_w = pltpu.make_async_copy(wcols(zl, c), wpiece(h, zl, c), rsem.at[local + 3])
    own_w.start()
    for n, off in enumerate(GROUP):
        dev = peer(*off)
        send(wcols(dev[1], dev[4]), wpiece(h, zl, c), PLAN["wg"] + n, dev)

    chip = h * NZ + zl
    sibling = (h, zl, y, x, 1 - c)

    def turn(by):
        return lax.rem(chip + 2 * NCHIP + by, NCHIP)

    def next_chip(way):
        to = turn(way)
        return (lax.div(to, NZ), lax.rem(to, NZ), y, x, c)

    def rows_of(odd):
        return pl.ds(0, CUT[0]) if odd == 0 else pl.ds(CUT[0], CUT[1])

    def unit(odd, pair):
        start = SKIP + pair * TOK + (CUT[0] if odd else 0)
        return hid.at[pl.ds(pl.multiple_of(start, 16), CUT[odd]), :]

    def kept(odd, origin, core):
        return X.at[origin * NC + core, rows_of(odd)]

    def passing(odd, way, n):
        return X.at[NCHIP * NC + (0 if way == 1 else 2) + n, rows_of(odd)]

    def side_of(odd, way):
        side = lax.rem(chip + odd, NZ)
        return side if way == 1 else 1 - side

    def hid_sem(odd, way, step, high):
        return PLAN["hn", odd, way] + 2 * (step - 1) + high

    def own_pair(odd):
        return lax.div(turn(-odd), NZ)

    def far_unit(odd, way, high):
        side = side_of(odd, way)
        if way == 1:
            return unit(odd, lax.div(turn(side + 2 * high - odd), NZ))
        return unit(odd, lax.div(turn(-1 - side - 2 * high - odd), NZ))

    def hid_send(odd, way, step, high):
        side = side_of(odd, way)
        origin = turn(-way * (step - 1))
        at_next = kept(odd, origin, c)
        when = None
        if step == 1:
            src = far_unit(odd, way, high)
            dst = passing(odd, way, 0) if high else at_next
        elif step == 2:
            src = passing(odd, way, 0) if high else kept(odd, origin, c)
            dst = at_next
            if high:
                dst = X.at[
                    jnp.where(side == 0, NCHIP * NC + (0 if way == 1 else 2) + 1, origin * NC + c), rows_of(odd)
                ]
            else:
                when = side == 0
        elif step == 3:
            src = X.at[jnp.where(side == 1, NCHIP * NC + (0 if way == 1 else 2) + 1, origin * NC + c), rows_of(odd)]
            dst = at_next
        else:
            src, dst, when = kept(odd, origin, c), at_next, side == 0
        send(src, dst, hid_sem(odd, way, step, high), next_chip(way), when=when)

    def share_unit(odd, n, origin):
        ref = kept(odd, origin, c)
        send(ref, ref, PLAN["hd", odd] + n, sibling)

    ORIGINS = (0, -1, 1, -2, 2, -3, 3, 4)

    def hid_take(odd, way, step, high):
        side = side_of(odd, way)
        origin = turn(-way * step)
        sem = hid_sem(odd, way, step, high)
        n = ORIGINS.index(-way * step) if step < 4 else 7
        ref = kept(odd, origin, c)
        if step == 1 and high:
            arrived(passing(odd, way, 0), sem)
            hid_send(odd, way, 2, 1)
        elif step == 1:
            arrived(ref, sem)
            hid_send(odd, way, 2, 0)
            share_unit(odd, n, origin)
        elif step == 2 and high:
            arrived(ref, sem)
            hid_send(odd, way, 3, 1)
        elif step == 2:
            arrived(ref, sem, side == 1)
            share_unit(odd, n, origin)
        elif step == 3:
            arrived(ref, sem)
            hid_send(odd, way, 4, 1)
            share_unit(odd, n, origin)
        else:
            arrived(ref, sem, side == 1)

    def takes(step, high):
        for odd in (1, 0):
            for way in (1, -1):
                hid_take(odd, way, step, high)
        if step == 4:
            for odd in (1, 0):
                share_unit(odd, 7, turn(4))

    own_x = []
    for odd in range(2):
        keep = pltpu.make_async_copy(unit(odd, own_pair(odd)), kept(odd, chip, c), rsem.at[local + 4 + odd])
        keep.start()
        own_x.append(keep)
    for high in (1, 0):
        for odd in (1, 0):
            for way in (1, -1):
                hid_send(odd, way, 1, high)
    for odd in range(2):
        send(unit(odd, own_pair(odd)), kept(odd, chip, c), PLAN["hd", odd], sibling)

    MSG[h, p] = jnp.zeros((8, COLS), jnp.float32)
    SS[...] = jnp.zeros_like(SS)
    SL[...] = jnp.zeros_like(SL)
    for fetch in fetches:
        fetch.wait()
    heads_wide = HEAD[...].astype(jnp.float32)
    for target in range(SEQ):
        for k in range(4):
            SAY[target, k : k + 1, :] = REFL[0:1, k * COLS : (k + 1) * COLS]
        for k in range(2):
            SAY[target, 4 + k : 5 + k, :] = jnp.full((1, COLS), SPANS[0, k], jnp.int32).astype(jnp.float32)
        SAY[target, 6:7, :] = heads_wide[:, target * COLS : (target + 1) * COLS]
        SAY[target, 7:8, :] = jnp.zeros((1, COLS), jnp.float32)
    SIDE[h, p] = SAY[p]
    for n, off in enumerate(GROUP):
        dev = peer(*off)
        send(SAY.at[dev[1] * NC + dev[4]], SIDE.at[h, p], PLAN["sd"] + n, dev)

    def settle(odd, which):
        for n in which:
            if n == 0:
                own_x[odd].wait()
            origin = turn(ORIGINS[n])
            block, low = lax.div(origin, NZ), lax.rem(origin, NZ)
            arrived(kept(odd, origin, 1 - c), PLAN["hd", odd] + n)
            first = 0 if odd == 0 else CUT[0]
            both = X[pl.ds(origin * NC, NC), first : first + CUT[odd], :]
            wide = both.astype(jnp.float32)
            wide = wide * wide
            part = wide[:, :, :COLS]
            for k in range(1, FB // COLS):
                part += wide[:, :, k * COLS : (k + 1) * COLS]
            SS[pl.ds(low * NC, NC), first : first + CUT[odd], :] += part
            flat = both.reshape(NC * CUT[odd], FB)
            if NC * CUT[odd] < COLS:
                flat = jnp.concatenate([flat, jnp.zeros((COLS - NC * CUT[odd], FB), jnp.bfloat16)], axis=0)
            lanes = pl.ds(pl.multiple_of((odd * NZ + low) * COLS, COLS), COLS)
            XT[block, :, lanes] = flat.T

    def piece(part, axis, half, pos):
        if part == "A":
            slabs = pl.ds(0, 2 - half)
        else:
            slabs = pl.ds(2 - half, 2 + half)
        if part == "A":
            if axis == "x":
                return W.at[slabs, half * NY + y, pos]
            return W.at[slabs, half * NY + pos]
        if axis == "y":
            return W.at[slabs, half * NY + pos, x]
        return W.at[slabs, pl.ds(half * NY, NY), pos]

    def gather_start(part, axis):
        for half, sign, _ in chains(NX if axis == "x" else NY):
            own = piece(part, axis, half, place(axis, 0))
            send(own, own, PLAN["ag", part, axis, half, sign], ring(axis, sign))

    def gather_step(part, axis, step):
        for half, sign, steps in chains(NX if axis == "x" else NY):
            if step > steps:
                continue
            base = PLAN["ag", part, axis, half, sign]
            got = piece(part, axis, half, place(axis, -sign * step))
            arrived(got, base + step - 1)
            if step < steps:
                send(got, got, base + step, ring(axis, sign))
            if part == "B":
                across_start(half, (-sign * step) % NY)

    def cell(half, by, pos):
        return W.at[pl.ds(2 - half, 2 + half), half * NY + place("y", by), pos]

    def across_start(half, by):
        for other, sign, steps in chains(NX):
            if other == half:
                own = cell(half, by, x)
                send(own, own, PLAN["ag", "B", "x", half, sign] + by * steps, ring("x", sign))

    def across_step(by, step):
        for half, sign, steps in chains(NX):
            if step > steps:
                continue
            base = PLAN["ag", "B", "x", half, sign] + by * steps
            got = cell(half, by, place("x", -sign * step))
            arrived(got, base + step - 1)
            if step < steps:
                send(got, got, base + step, ring("x", sign))

    own_w.wait()
    for n, off in enumerate(GROUP):
        arrived(wpiece(*origin(*off)), PLAN["wg"] + n)
    gather_start("A", "x")
    gather_start("B", "y")
    for half in range(NZ):
        across_start(half, 0)
    takes(1, 1)
    gather_step("A", "x", 1)
    gather_step("B", "y", 1)
    gather_step("A", "x", 2)
    gather_start("A", "y")
    across_step(0, 1)
    gather_step("B", "y", 2)
    takes(1, 0)
    across_step(1, 1)
    across_step(7, 1)
    gather_step("B", "y", 3)
    takes(2, 1)
    across_step(0, 2)
    across_step(2, 1)
    across_step(6, 1)
    gather_step("B", "y", 4)
    gather_step("A", "y", 1)
    takes(2, 0)
    for odd in range(2):
        settle(odd, (0, 1, 2))
    across_step(1, 2)
    across_step(7, 2)
    across_step(3, 1)
    across_step(5, 1)
    gather_step("A", "y", 2)
    takes(3, 1)
    across_step(2, 2)
    across_step(6, 2)
    across_step(4, 1)
    for odd in range(2):
        settle(odd, (3, 4))
    gather_step("A", "y", 3)
    across_step(3, 2)
    across_step(5, 2)
    takes(4, 1)
    across_step(4, 2)
    gather_step("A", "y", 4)
    for odd in range(2):
        settle(odd, (5, 6, 7))
    for n, off in enumerate(GROUP):
        hs, zs, cs = origin(*off)
        arrived(SIDE.at[hs, zs * NC + cs], PLAN["sd"] + n)

    ACC[...] = jnp.zeros_like(ACC)

    def project(j, carry):
        tokens = X[pl.ds(4 * j, 4)].reshape(ROWS, FB)
        for k in range(2):
            sides = [W[2 * k + e, pl.ds(4 * j, 4)].reshape(FB, COLS) for e in range(2)]
            both = jnp.concatenate(sides, axis=1)
            product = jnp.dot(tokens, both, preferred_element_type=jnp.float32)
            ACC[:, :, 2 * COLS * k : 2 * COLS * (k + 1)] += product.reshape(SEQ, TOK, 2 * COLS)
        return carry

    lax.fori_loop(0, NH, project, 0)

    heads = [SIDE[s, p, 6:7, :] for s in range(4)]
    ones = jnp.ones((8, COLS), jnp.float32)

    def row_sums(values):
        sums = lax.dot_general(
            ones, values, (((1,), (1,)), ((), ())), precision=HIGHEST, preferred_element_type=jnp.float32
        )
        return sums[0:1, :]

    lane = lax.broadcasted_iota(jnp.int32, (1, COLS), 1)
    blocks = (h, lax.rem(h + 3 + zl, NH))
    at_lane = (lane + SKIP + TOK * jnp.where(lane < CUT[0], blocks[0], blocks[1])).astype(jnp.float32)[:, :TOK]
    for i in range(SEQ):
        starts, ending = SIDE[h, i, 4:5, 0:TOK], SIDE[h, i, 5:6, 0:TOK]
        inside = jnp.where((at_lane >= starts) & (at_lane < ending), 1.0, 0.0)
        last_tok = jnp.where(at_lane == ending - 1.0, 1.0, 0.0)
        meansq = jnp.sum(SS[i], axis=1, keepdims=True) * (1.0 / D)
        scale = lax.rsqrt(meansq + NORM_EPS)
        weighted = []
        for s in range(4):
            raw = ACC[i, :, s * COLS : (s + 1) * COLS] * scale
            pre = raw.astype(jnp.bfloat16).astype(jnp.float32)
            sigmoid = 1.0 / (1.0 + jnp.exp(-pre))
            weighted.append(heads[s] * (pre * sigmoid))
            if s < 2:
                slope = sigmoid * (1.0 + pre * (1.0 - sigmoid))
                ACC[i, :, s * COLS : (s + 1) * COLS] = scale * heads[s] * slope
        log_prob = row_sums(weighted[0] + weighted[1])
        MSG[h, p, i : i + 1, 0:TOK] = -KL_COEF * log_prob * inside + row_sums(weighted[3]) * last_tok
        MSG[h, p, 4 + i : 5 + i, 0:TOK] = row_sums(weighted[2])
    for n, off in enumerate(GROUP):
        send(MSG.at[h, p], MSG.at[h, p], PLAN["mg"] + n, peer(*off))

    for i in range(SEQ):
        for k in range(4):
            part = slice(k * COLS, (k + 1) * COLS)
            ROWS4[0, i : i + 1, part] = SIDE[h, i, k : k + 1, :]
            ROWS4[1, i : i + 1, part] = SIDE[h, i, 4:5, :]
            ROWS4[2, i : i + 1, part] = SIDE[h, i, 5:6, :]
    for n, off in enumerate(GROUP):
        hs, zs, cs = origin(*off)
        arrived(MSG.at[hs, zs * NC + cs], PLAN["mg"] + n)

    whole = jnp.zeros((8, LEN), jnp.float32)
    for a in range(NH):
        nxt = (a + 1) % NH
        early = jnp.where(lane < CUT[0], MSG[a, 0] + MSG[a, 1], MSG[nxt, 0] + MSG[nxt, 1])
        total = early + (MSG[a, 2] + MSG[a, 3])
        wide = jnp.concatenate([total, jnp.zeros((8, LEN - COLS), jnp.float32)], axis=1)
        whole += pltpu.roll(wide, SKIP + a * TOK, 1)
    gains, value_est = whole[0:4], whole[4:8]
    position = lax.broadcasted_iota(jnp.int32, (SEQ, LEN), 1)
    ref, starts, ending = ROWS4[0, 0:4, :], ROWS4[1, 0:4, :], ROWS4[2, 0:4, :]
    at = position.astype(jnp.float32)
    inside = jnp.where((at >= starts) & (at < ending), 1.0, 0.0)
    follow = jnp.where(at + 1.0 < ending, 1.0, 0.0)
    reward = gains + KL_COEF * ref * inside
    next_value = pltpu.roll(value_est, LEN - 1, 1)
    trail = (reward + DISCOUNT * next_value * follow - value_est) * inside
    span = 1
    while span < LEN:
        later = jnp.where(position + span < LEN, pltpu.roll(trail, LEN - span, 1), 0.0)
        trail += (DISCOUNT * TRACE_DECAY) ** span * later
        span *= 2
    advantage = trail * inside
    signal = -advantage / (ending - starts)
    mine = lax.broadcasted_iota(jnp.int32, (SEQ, LEN), 0) == p
    adv_out[...] = jnp.sum(jnp.where(mine, advantage, 0.0), axis=0, keepdims=True)

    near = jnp.zeros((SEQ, COLS), jnp.float32)
    for a in range(NH):
        turned = pltpu.roll(signal, LEN - SKIP - a * TOK, 1)[:, :COLS]
        wanted = jnp.where(lane < CUT[0], blocks[0], blocks[1]) == a
        near += jnp.where(wanted, turned, 0.0)
    square = jnp.concatenate([near, jnp.zeros((COLS - SEQ, COLS), jnp.float32)], axis=0).T
    for i in range(SEQ):
        factor = square[0:TOK, i : i + 1]
        slopes = (factor * ACC[i, :, 0 : 2 * COLS]).astype(jnp.bfloat16)
        low, core = i // NC, i % NC
        for odd in range(2):
            first = (odd * NZ + low) * COLS + core * CUT[odd]
            taken = slice(0, CUT[0]) if odd == 0 else slice(CUT[0], TOK)
            SL[first : first + CUT[odd], :] = slopes[taken]

    def share(half, pos):
        block = half * NY + lax.rem(pos + 2 * NY, NY)
        j = lax.div(block, 4)
        features = pl.ds(pl.multiple_of(lax.rem(block, 4) * 256, 256), 256)
        product = jnp.dot(XT[j, features, :], SL[...], preferred_element_type=jnp.float32)
        G[0, block] = product[:, :COLS].reshape(NX, 64, COLS)
        G[1, block] = product[:, COLS:].reshape(NX, 64, COLS)

    def at_of(part, axis, half, pos, sub=None):
        if part == "A":
            if axis == "x":
                return (0, half * NY + y, pos)
            return (0, half * NY + pos, pl.ds(2 * sub, 2))
        if axis == "x":
            return (1, pl.ds(half * NY + 4 * sub, 4), pos)
        return (1, half * NY + pos, x)

    def room(buf, part, axis, sid):
        return buf[part, axis].at[sid - PLAN["rs", part, axis, 0, 0, 1]]

    def sum_send(part, axis, sub, half, sign, steps, step):
        sid = PLAN["rs", part, axis, sub, half, sign] + step - 1
        own = G[at_of(part, axis, half, place(axis, sign * (steps + 1 - step)), sub)]
        if step > 1:
            own += room(LAND, part, axis, sid - 1)[...].astype(jnp.float32)
        stage = room(STAGE, part, axis, sid)
        stage[...] = own.astype(jnp.bfloat16)
        send(stage, room(LAND, part, axis, sid), sid, ring(axis, sign))

    def sum_step(part, axis, step, sub, only=None):
        for half, sign, steps in chains(NX if axis == "x" else NY):
            if step > steps or (only is not None and steps != only):
                continue
            sid = PLAN["rs", part, axis, sub, half, sign] + step - 1
            arrived(room(LAND, part, axis, sid), sid)
            if step == steps:
                mine_at = at_of(part, axis, half, place(axis, 0), sub)
                G[mine_at] = G[mine_at] + room(LAND, part, axis, sid)[...].astype(jnp.float32)
            else:
                sum_send(part, axis, sub, half, sign, steps, step + 1)

    def direct_send(part, axis):
        size = NX if axis == "x" else NY
        for by in sorted(range(1, size), key=lambda d: -min(d, size - d)):
            for half in range(NZ):
                n = half * (size - 1) + by - 1
                stage = STAGE[part, axis].at[n]
                stage[...] = G[at_of(part, axis, half, place(axis, by))].astype(jnp.bfloat16)
                send(stage, LAND[part, axis].at[n], PLAN["direct", axis] + n, ring(axis, by))

    def direct_take(part, axis, k):
        size = NX if axis == "x" else NY
        for half in range(NZ):
            total = G[at_of(part, axis, half, place(axis, 0))]
            for by in range(1, size):
                n = half * (size - 1) + by - 1
                arrived(LAND[part, axis].at[n], PLAN["direct", axis] + n)
                total += LAND[part, axis][n].astype(jnp.float32)
            FIN[k, half] = total.astype(jnp.bfloat16)

    for half, sign, steps in chains(NY):
        share(half, y + sign * steps)
        sum_send("A", "y", 0, half, sign, steps, 1)
    for half, sign, steps in chains(NY):
        sum_send("A", "y", 1, half, sign, steps, 1)

    def shares(n, carry):
        share(0, y + 3 - n)
        share(1, y - 3 + n)
        return carry

    lax.fori_loop(0, NY - 2, shares, 0)
    for long in (2, 1):
        for sub in range(2):
            for half, sign, steps in chains(NX):
                if steps == long:
                    sum_send("B", "x", sub, half, sign, steps, 1)
    for sub in range(2):
        sum_step("A", "y", 1, sub)
    for sub in range(2):
        sum_step("B", "x", 1, sub, only=2)
    for sub in range(2):
        sum_step("A", "y", 2, sub)
    for sub in range(2):
        sum_step("A", "y", 3, sub)
    for sub in range(2):
        sum_step("B", "x", 1, sub, only=1)
    for sub in range(2):
        sum_step("B", "x", 2, sub)
    direct_send("B", "y")
    for sub in range(2):
        sum_step("A", "y", 4, sub)
    direct_send("A", "x")

    handed = []
    for k, part, axis in ((1, "B", "y"), (0, "A", "x")):
        direct_take(part, axis, k)
        for half in range(NZ):
            for core in range(NC):
                dest_h = k + 2 * zl
                src = FIN.at[k, half, pl.ds(core * 32, 32), :]
                dst = FR.at[h, c]
                rid = PLAN["fn"] + h * NC + c
                sid = PLAN["fn"] + (k * NZ + half) * NC + core
                here = (dest_h == h) & (half == zl) & (core == c)
                remote = pltpu.make_async_remote_copy(
                    src_ref=src,
                    dst_ref=dst,
                    send_sem=ssem.at[sid],
                    recv_sem=rsem.at[rid],
                    device_id=(dest_h, half, y, x, core),
                    device_id_type=MESH,
                )
                keep = pltpu.make_async_copy(src, dst, rsem.at[rid])
                pl.when(here)(keep.start)
                pl.when(jnp.logical_not(here))(remote.start)
                handed.append((here, remote))
    for a in range(NH):
        for core in range(NC):
            arrived(FR.at[a, core], PLAN["fn"] + a * NC + core)
    for core in range(NC):
        parts = [FR[a, core].astype(jnp.float32) for a in range(NH)]
        grad_out[0, :, core * COLS : (core + 1) * COLS] = (parts[0] + parts[1]) + (parts[2] + parts[3])
    for here, remote in handed:
        pl.when(jnp.logical_not(here))(remote.wait_send)
    for when, copy in pend:
        if when is None:
            copy.wait_send()
        else:
            pl.when(when)(copy.wait_send)


def shards(hidden, window_proj, head_weights, ref_logprob, resp_spans):
    vmem = pl.BlockSpec(memory_space=pltpu.VMEM)
    hbm = pl.BlockSpec(memory_space=pl.ANY)
    bf16, f32 = jnp.bfloat16, jnp.float32
    rooms = {
        ("A", "y"): pltpu.VMEM((28, NX // 2, 64, COLS), bf16),
        ("A", "x"): pltpu.VMEM((6, 64, COLS), bf16),
        ("B", "x"): pltpu.VMEM((12, NY // 2, 64, COLS), bf16),
        ("B", "y"): pltpu.VMEM((14, 64, COLS), bf16),
    }
    return pl.pallas_call(
        kernel,
        out_shape=(
            jax.ShapeDtypeStruct((1, 32, 2 * COLS), f32),
            jax.ShapeDtypeStruct((1, LEN), f32),
        ),
        in_specs=[hbm] * 5,
        out_specs=(vmem, vmem),
        scratch_shapes=[
            pltpu.VMEM((NCHIP * NC + 4, TOK, FB), bf16),
            pltpu.VMEM((NH, FB, 4 * COLS), bf16),
            pltpu.VMEM((4, NZ * NY, NX, 64, COLS), bf16),
            pltpu.VMEM((SEQ, 8, COLS), f32),
            pltpu.VMEM((NH, SEQ, 8, COLS), f32),
            pltpu.VMEM((NH, SEQ, 8, COLS), f32),
            pltpu.VMEM((SEQ, TOK, COLS), f32),
            pltpu.VMEM((SEQ, TOK, 4 * COLS), f32),
            pltpu.VMEM((4 * COLS, 2 * COLS), bf16),
            pltpu.VMEM((2, NZ * NY, NX, 64, COLS), f32),
            pltpu.VMEM((3, 8, LEN), f32),
            rooms,
            rooms,
            pltpu.VMEM((2, NZ, 64, COLS), bf16),
            pltpu.VMEM((NH, NC, 32, COLS), bf16),
            pltpu.VMEM((1, LEN), bf16),
            pltpu.VMEM((1, LEN), f32),
            pltpu.SMEM((1, 2), jnp.int32),
            pltpu.SemaphoreType.DMA((PLAN["total"],)),
            pltpu.SemaphoreType.DMA((PLAN["total"],)),
        ],
        compiler_params=pltpu.CompilerParams(
            collective_id=0, has_side_effects=True, vmem_limit_bytes=60 * 1024 * 1024
        ),
    )(hidden, window_proj, head_weights, ref_logprob, resp_spans)


def solution(mesh):
    finer = Mesh(mesh.devices.reshape(NH, NZ, NY, NX, NC), AXES)
    return jax.shard_map(
        shards,
        mesh=finer,
        in_specs=(P(FSDP, "h"), P("h", FSDP, None), P("h", None), P(FSDP, None), P(FSDP, None)),
        out_specs=(P("h", FSDP, None), P(FSDP, None)),
        check_vma=False,
    )
```

```python
import jax
import jax.numpy as jnp
from jax import lax
from jax.experimental import pallas as pl
from jax.experimental.pallas import tpu as pltpu
from jax.sharding import Mesh
from jax.sharding import PartitionSpec as P

AXES = ("h", "zl", "y", "x", "c")
FSDP = AXES[1:]
MESH = pl.DeviceIdType.MESH

NH, NZ, NY, NX, NC = 4, 2, 8, 4, 2
LEN = 512
SKIP = 64
TOK = (LEN - SKIP) // NH
CUT = (48, 64)
SEQ = NZ * NC
ROWS = SEQ * TOK
FB = 1024
COLS = 128
D = NH * FB
NCHIP = NH * NZ

KL_COEF = 0.1
DISCOUNT = 1.0
TRACE_DECAY = 0.95
NORM_EPS = 1e-05
HIGHEST = lax.Precision.HIGHEST

GROUP = [(a, b, e) for a in (2, 1, 3, 0) for b in range(NZ) for e in range(NC) if (a, b, e) != (0, 0, 0)]


def chains(size):
    far, near = size // 2, size // 2 - 1
    return [(0, 1, far), (1, -1, far), (0, -1, near), (1, 1, near)]


def plan():
    out = {}
    used = 0

    def take(name, count):
        nonlocal used
        out[name] = used
        used += count

    for name in ("wg", "sd", "mg"):
        take(name, len(GROUP))
    for odd in range(2):
        for way in (1, -1):
            take(("hn", odd, way), 8)
        take(("hd", odd), 8)
    for part, axis in (("A", "x"), ("B", "y")):
        for half, sign, steps in chains(NX if axis == "x" else NY):
            take(("ag", part, axis, half, sign), steps)
    for sub in range(2):
        for half, sign, steps in chains(NY):
            take(("ag", "A", "y", sub, half, sign), steps)
    for half, sign, steps in chains(NX):
        take(("ag", "B", "x", half, sign), steps * NY)
    for part, axis in (("A", "y"), ("B", "x")):
        for sub in range(2):
            for half, sign, steps in chains(NX if axis == "x" else NY):
                take(("rs", part, axis, sub, half, sign), steps)
    take(("direct", "x"), NZ * (NX - 1))
    take(("direct", "y"), NZ * (NY - 1))
    take("fn", NH * NC)
    take("local", 8)
    out["total"] = used
    return out


PLAN = plan()


def kernel(
    hid, win, head_in, refl_in, spans_in, grad_out, adv_out,
    X, XT, W, SAY, SIDE, MSG, SS, ACC, SL, G, ROWS4, STAGE, LAND, FIN, FR, HEAD, REFL, SPANS,
    ssem, rsem,
):
    h, zl, y, x, c = (lax.axis_index(a) for a in AXES)
    p = zl * NC + c
    pend = []

    def send(src, dst, sid, dev, rid=None, when=None):
        copy = pltpu.make_async_remote_copy(
            src_ref=src,
            dst_ref=dst,
            send_sem=ssem.at[sid],
            recv_sem=rsem.at[sid if rid is None else rid],
            device_id=dev,
            device_id_type=MESH,
        )
        if when is None:
            copy.start()
        else:
            pl.when(when)(copy.start)
        pend.append((when, copy))

    def arrived(ref, sid, when=None):
        copy = pltpu.make_async_copy(ref, ref, rsem.at[sid])
        if when is None:
            copy.wait()
        else:
            pl.when(when)(copy.wait)

    def peer(dh, dz, dc):
        return (lax.rem(h + dh, NH), lax.rem(zl + dz, NZ), y, x, lax.rem(c + dc, NC))

    def origin(dh, dz, dc):
        return (lax.rem(h + NH - dh, NH), lax.rem(zl + NZ - dz, NZ), lax.rem(c + NC - dc, NC))

    def place(axis, by):
        return lax.rem(x + 2 * NX + by, NX) if axis == "x" else lax.rem(y + 2 * NY + by, NY)

    def ring(axis, by):
        if axis == "x":
            return (h, zl, y, place("x", by), c)
        return (h, zl, place("y", by), x, c)

    barrier = pltpu.get_barrier_semaphore()
    mates = [peer(*o) for o in GROUP]
    mates += [ring("x", by) for by in range(1, NX)] + [ring("y", by) for by in range(1, NY)]
    for dev in mates:
        pl.semaphore_signal(barrier, inc=1, device_id=dev, device_id_type=MESH)
    local = PLAN["local"]
    fetches = [
        pltpu.make_async_copy(src, dst, rsem.at[local + n])
        for n, (src, dst) in enumerate(((head_in, HEAD), (refl_in, REFL), (spans_in, SPANS)))
    ]
    for fetch in fetches:
        fetch.start()
    pl.semaphore_wait(barrier, len(mates))

    def wpiece(hs, zs, cs):
        return W.at[hs, zs * NY + y, x, pl.ds(pl.multiple_of(cs * 32, 32), 32), :]

    def wcols(zs, cs):
        return win.at[0, :, pl.ds(pl.multiple_of((zs * NC + cs) * COLS, COLS), COLS)]

    own_w = pltpu.make_async_copy(wcols(zl, c), wpiece(h, zl, c), rsem.at[local + 3])
    own_w.start()
    for n, off in enumerate(GROUP):
        dev = peer(*off)
        send(wcols(dev[1], dev[4]), wpiece(h, zl, c), PLAN["wg"] + n, dev)

    chip = h * NZ + zl
    sibling = (h, zl, y, x, 1 - c)

    def turn(by):
        return lax.rem(chip + 2 * NCHIP + by, NCHIP)

    def next_chip(way):
        to = turn(way)
        return (lax.div(to, NZ), lax.rem(to, NZ), y, x, c)

    def rows_of(odd):
        return pl.ds(0, CUT[0]) if odd == 0 else pl.ds(CUT[0], CUT[1])

    def unit(odd, pair):
        start = SKIP + pair * TOK + (CUT[0] if odd else 0)
        return hid.at[pl.ds(pl.multiple_of(start, 16), CUT[odd]), :]

    def kept(odd, origin, core):
        return X.at[origin * NC + core, rows_of(odd)]

    def passing(odd, way, n):
        return X.at[NCHIP * NC + (0 if way == 1 else 2) + n, rows_of(odd)]

    def side_of(odd, way):
        side = lax.rem(chip + odd, NZ)
        return side if way == 1 else 1 - side

    def hid_sem(odd, way, step, high):
        return PLAN["hn", odd, way] + 2 * (step - 1) + high

    def own_pair(odd):
        return lax.div(turn(-odd), NZ)

    def far_unit(odd, way, high):
        side = side_of(odd, way)
        if way == 1:
            return unit(odd, lax.div(turn(side + 2 * high - odd), NZ))
        return unit(odd, lax.div(turn(-1 - side - 2 * high - odd), NZ))

    def hid_send(odd, way, step, high):
        side = side_of(odd, way)
        origin = turn(-way * (step - 1))
        at_next = kept(odd, origin, c)
        when = None
        if step == 1:
            src = far_unit(odd, way, high)
            dst = passing(odd, way, 0) if high else at_next
        elif step == 2:
            src = passing(odd, way, 0) if high else kept(odd, origin, c)
            dst = at_next
            if high:
                dst = X.at[
                    jnp.where(side == 0, NCHIP * NC + (0 if way == 1 else 2) + 1, origin * NC + c), rows_of(odd)
                ]
            else:
                when = side == 0
        elif step == 3:
            src = X.at[jnp.where(side == 1, NCHIP * NC + (0 if way == 1 else 2) + 1, origin * NC + c), rows_of(odd)]
            dst = at_next
        else:
            src, dst, when = kept(odd, origin, c), at_next, side == 0
        send(src, dst, hid_sem(odd, way, step, high), next_chip(way), when=when)

    def share_unit(odd, n, origin):
        ref = kept(odd, origin, c)
        send(ref, ref, PLAN["hd", odd] + n, sibling)

    ORIGINS = (0, -1, 1, -2, 2, -3, 3, 4)

    def hid_take(odd, way, step, high):
        side = side_of(odd, way)
        origin = turn(-way * step)
        sem = hid_sem(odd, way, step, high)
        n = ORIGINS.index(-way * step) if step < 4 else 7
        ref = kept(odd, origin, c)
        if step == 1 and high:
            arrived(passing(odd, way, 0), sem)
            hid_send(odd, way, 2, 1)
        elif step == 1:
            arrived(ref, sem)
            hid_send(odd, way, 2, 0)
            share_unit(odd, n, origin)
        elif step == 2 and high:
            arrived(ref, sem)
            hid_send(odd, way, 3, 1)
        elif step == 2:
            arrived(ref, sem, side == 1)
            share_unit(odd, n, origin)
        elif step == 3:
            arrived(ref, sem)
            hid_send(odd, way, 4, 1)
            share_unit(odd, n, origin)
        else:
            arrived(ref, sem, side == 1)

    def takes(step, high):
        for odd in (1, 0):
            for way in (1, -1):
                hid_take(odd, way, step, high)
        if step == 4:
            for odd in (1, 0):
                share_unit(odd, 7, turn(4))

    own_x = []
    for odd in range(2):
        keep = pltpu.make_async_copy(unit(odd, own_pair(odd)), kept(odd, chip, c), rsem.at[local + 4 + odd])
        keep.start()
        own_x.append(keep)
    for high in (1, 0):
        for odd in (1, 0):
            for way in (1, -1):
                hid_send(odd, way, 1, high)
    for odd in range(2):
        send(unit(odd, own_pair(odd)), kept(odd, chip, c), PLAN["hd", odd], sibling)

    MSG[h, p] = jnp.zeros((8, COLS), jnp.float32)
    SS[...] = jnp.zeros_like(SS)
    SL[...] = jnp.zeros_like(SL)
    for fetch in fetches:
        fetch.wait()
    heads_wide = HEAD[...].astype(jnp.float32)
    for target in range(SEQ):
        for k in range(4):
            SAY[target, k : k + 1, :] = REFL[0:1, k * COLS : (k + 1) * COLS]
        for k in range(2):
            SAY[target, 4 + k : 5 + k, :] = jnp.full((1, COLS), SPANS[0, k], jnp.int32).astype(jnp.float32)
        SAY[target, 6:7, :] = heads_wide[:, target * COLS : (target + 1) * COLS]
        SAY[target, 7:8, :] = jnp.zeros((1, COLS), jnp.float32)
    SIDE[h, p] = SAY[p]
    for n, off in enumerate(GROUP):
        dev = peer(*off)
        send(SAY.at[dev[1] * NC + dev[4]], SIDE.at[h, p], PLAN["sd"] + n, dev)

    def settle(odd, which):
        for n in which:
            if n == 0:
                own_x[odd].wait()
            origin = turn(ORIGINS[n])
            block, low = lax.div(origin, NZ), lax.rem(origin, NZ)
            arrived(kept(odd, origin, 1 - c), PLAN["hd", odd] + n)
            first = 0 if odd == 0 else CUT[0]
            both = X[pl.ds(origin * NC, NC), first : first + CUT[odd], :]
            wide = both.astype(jnp.float32)
            wide = wide * wide
            part = wide[:, :, :COLS]
            for k in range(1, FB // COLS):
                part += wide[:, :, k * COLS : (k + 1) * COLS]
            SS[pl.ds(low * NC, NC), first : first + CUT[odd], :] += part
            flat = both.reshape(NC * CUT[odd], FB)
            if NC * CUT[odd] < COLS:
                flat = jnp.concatenate([flat, jnp.zeros((COLS - NC * CUT[odd], FB), jnp.bfloat16)], axis=0)
            lanes = pl.ds(pl.multiple_of((odd * NZ + low) * COLS, COLS), COLS)
            XT[block, :, lanes] = flat.T

    def piece(part, axis, half, pos):
        if part == "A":
            slabs = pl.ds(0, 2 - half)
        else:
            slabs = pl.ds(2 - half, 2 + half)
        if part == "A":
            if axis == "x":
                return W.at[slabs, half * NY + y, pos]
            return W.at[slabs, half * NY + pos]
        if axis == "y":
            return W.at[slabs, half * NY + pos, x]
        return W.at[slabs, pl.ds(half * NY, NY), pos]

    def gather_start(part, axis):
        for half, sign, _ in chains(NX if axis == "x" else NY):
            own = piece(part, axis, half, place(axis, 0))
            send(own, own, PLAN["ag", part, axis, half, sign], ring(axis, sign))

    def gather_step(part, axis, step):
        for half, sign, steps in chains(NX if axis == "x" else NY):
            if step > steps:
                continue
            base = PLAN["ag", part, axis, half, sign]
            got = piece(part, axis, half, place(axis, -sign * step))
            arrived(got, base + step - 1)
            if step < steps:
                send(got, got, base + step, ring(axis, sign))
            if part == "B":
                across_start(half, (-sign * step) % NY)

    def along(half, by, sub):
        return W.at[pl.ds(0, 2 - half), half * NY + place("y", by), pl.ds(2 * sub, 2)]

    def along_start(sub):
        for half, sign, _ in chains(NY):
            own = along(half, 0, sub)
            send(own, own, PLAN["ag", "A", "y", sub, half, sign], ring("y", sign))

    def along_step(step):
        for sub in range(2):
            for half, sign, steps in chains(NY):
                if step > steps:
                    continue
                base = PLAN["ag", "A", "y", sub, half, sign]
                got = along(half, -sign * step, sub)
                arrived(got, base + step - 1)
                if step < steps:
                    send(got, got, base + step, ring("y", sign))

    def cell(half, by, pos):
        return W.at[pl.ds(2 - half, 2 + half), half * NY + place("y", by), pos]

    def across_start(half, by):
        for other, sign, steps in chains(NX):
            if other == half:
                own = cell(half, by, x)
                send(own, own, PLAN["ag", "B", "x", half, sign] + by * steps, ring("x", sign))

    def across_step(by, step):
        for half, sign, steps in chains(NX):
            if step > steps:
                continue
            base = PLAN["ag", "B", "x", half, sign] + by * steps
            got = cell(half, by, place("x", -sign * step))
            arrived(got, base + step - 1)
            if step < steps:
                send(got, got, base + step, ring("x", sign))

    own_w.wait()
    for n, off in enumerate(GROUP):
        arrived(wpiece(*origin(*off)), PLAN["wg"] + n)
    gather_start("A", "x")
    gather_start("B", "y")
    for half in range(NZ):
        across_start(half, 0)
    takes(1, 1)
    gather_step("A", "x", 1)
    gather_step("B", "y", 1)
    gather_step("A", "x", 2)
    for sub in range(2):
        along_start(sub)
    across_step(0, 1)
    gather_step("B", "y", 2)
    gather_step("B", "y", 3)
    takes(1, 0)
    across_step(1, 1)
    across_step(7, 1)
    gather_step("B", "y", 4)
    takes(2, 1)
    along_step(1)
    across_step(2, 1)
    across_step(6, 1)
    takes(2, 0)
    along_step(2)
    across_step(3, 1)
    across_step(5, 1)
    takes(3, 1)
    across_step(4, 1)
    along_step(3)
    takes(4, 1)
    for odd in range(2):
        settle(odd, (0, 1, 2,))
    for odd in range(2):
        settle(odd, (3, 4,))
    for odd in range(2):
        settle(odd, (5, 6, 7,))
    for by in range(NY):
        across_step(by, 2)
    along_step(4)
    for n, off in enumerate(GROUP):
        hs, zs, cs = origin(*off)
        arrived(SIDE.at[hs, zs * NC + cs], PLAN["sd"] + n)

    ACC[...] = jnp.zeros_like(ACC)

    def project(j, carry):
        tokens = X[pl.ds(4 * j, 4)].reshape(ROWS, FB)
        for k in range(2):
            sides = [W[2 * k + e, pl.ds(4 * j, 4)].reshape(FB, COLS) for e in range(2)]
            both = jnp.concatenate(sides, axis=1)
            product = jnp.dot(tokens, both, preferred_element_type=jnp.float32)
            ACC[:, :, 2 * COLS * k : 2 * COLS * (k + 1)] += product.reshape(SEQ, TOK, 2 * COLS)
        return carry

    lax.fori_loop(0, NH, project, 0)

    heads = [SIDE[s, p, 6:7, :] for s in range(4)]
    ones = jnp.ones((8, COLS), jnp.float32)

    def row_sums(values):
        sums = lax.dot_general(
            ones, values, (((1,), (1,)), ((), ())), precision=HIGHEST, preferred_element_type=jnp.float32
        )
        return sums[0:1, :]

    lane = lax.broadcasted_iota(jnp.int32, (1, COLS), 1)
    blocks = (h, lax.rem(h + 3 + zl, NH))
    at_lane = (lane + SKIP + TOK * jnp.where(lane < CUT[0], blocks[0], blocks[1])).astype(jnp.float32)[:, :TOK]
    for i in range(SEQ):
        starts, ending = SIDE[h, i, 4:5, 0:TOK], SIDE[h, i, 5:6, 0:TOK]
        inside = jnp.where((at_lane >= starts) & (at_lane < ending), 1.0, 0.0)
        last_tok = jnp.where(at_lane == ending - 1.0, 1.0, 0.0)
        meansq = jnp.sum(SS[i], axis=1, keepdims=True) * (1.0 / D)
        scale = lax.rsqrt(meansq + NORM_EPS)
        weighted = []
        for s in range(4):
            raw = ACC[i, :, s * COLS : (s + 1) * COLS] * scale
            pre = raw.astype(jnp.bfloat16).astype(jnp.float32)
            sigmoid = 1.0 / (1.0 + jnp.exp(-pre))
            weighted.append(heads[s] * (pre * sigmoid))
            if s < 2:
                slope = sigmoid * (1.0 + pre * (1.0 - sigmoid))
                ACC[i, :, s * COLS : (s + 1) * COLS] = scale * heads[s] * slope
        log_prob = row_sums(weighted[0] + weighted[1])
        MSG[h, p, i : i + 1, 0:TOK] = -KL_COEF * log_prob * inside + row_sums(weighted[3]) * last_tok
        MSG[h, p, 4 + i : 5 + i, 0:TOK] = row_sums(weighted[2])
    for n, off in enumerate(GROUP):
        send(MSG.at[h, p], MSG.at[h, p], PLAN["mg"] + n, peer(*off))

    for i in range(SEQ):
        for k in range(4):
            part = slice(k * COLS, (k + 1) * COLS)
            ROWS4[0, i : i + 1, part] = SIDE[h, i, k : k + 1, :]
            ROWS4[1, i : i + 1, part] = SIDE[h, i, 4:5, :]
            ROWS4[2, i : i + 1, part] = SIDE[h, i, 5:6, :]
    for n, off in enumerate(GROUP):
        hs, zs, cs = origin(*off)
        arrived(MSG.at[hs, zs * NC + cs], PLAN["mg"] + n)

    whole = jnp.zeros((8, LEN), jnp.float32)
    for a in range(NH):
        nxt = (a + 1) % NH
        early = jnp.where(lane < CUT[0], MSG[a, 0] + MSG[a, 1], MSG[nxt, 0] + MSG[nxt, 1])
        total = early + (MSG[a, 2] + MSG[a, 3])
        wide = jnp.concatenate([total, jnp.zeros((8, LEN - COLS), jnp.float32)], axis=1)
        whole += pltpu.roll(wide, SKIP + a * TOK, 1)
    gains, value_est = whole[0:4], whole[4:8]
    position = lax.broadcasted_iota(jnp.int32, (SEQ, LEN), 1)
    ref, starts, ending = ROWS4[0, 0:4, :], ROWS4[1, 0:4, :], ROWS4[2, 0:4, :]
    at = position.astype(jnp.float32)
    inside = jnp.where((at >= starts) & (at < ending), 1.0, 0.0)
    follow = jnp.where(at + 1.0 < ending, 1.0, 0.0)
    reward = gains + KL_COEF * ref * inside
    next_value = pltpu.roll(value_est, LEN - 1, 1)
    trail = (reward + DISCOUNT * next_value * follow - value_est) * inside
    span = 1
    while span < LEN:
        later = jnp.where(position + span < LEN, pltpu.roll(trail, LEN - span, 1), 0.0)
        trail += (DISCOUNT * TRACE_DECAY) ** span * later
        span *= 2
    advantage = trail * inside
    signal = -advantage / (ending - starts)
    mine = lax.broadcasted_iota(jnp.int32, (SEQ, LEN), 0) == p
    adv_out[...] = jnp.sum(jnp.where(mine, advantage, 0.0), axis=0, keepdims=True)

    near = jnp.zeros((SEQ, COLS), jnp.float32)
    for a in range(NH):
        turned = pltpu.roll(signal, LEN - SKIP - a * TOK, 1)[:, :COLS]
        wanted = jnp.where(lane < CUT[0], blocks[0], blocks[1]) == a
        near += jnp.where(wanted, turned, 0.0)
    square = jnp.concatenate([near, jnp.zeros((COLS - SEQ, COLS), jnp.float32)], axis=0).T
    for i in range(SEQ):
        factor = square[0:TOK, i : i + 1]
        slopes = (factor * ACC[i, :, 0 : 2 * COLS]).astype(jnp.bfloat16)
        low, core = i // NC, i % NC
        for odd in range(2):
            first = (odd * NZ + low) * COLS + core * CUT[odd]
            taken = slice(0, CUT[0]) if odd == 0 else slice(CUT[0], TOK)
            SL[first : first + CUT[odd], :] = slopes[taken]

    def share(half, pos):
        block = half * NY + lax.rem(pos + 2 * NY, NY)
        j = lax.div(block, 4)
        features = pl.ds(pl.multiple_of(lax.rem(block, 4) * 256, 256), 256)
        product = jnp.dot(XT[j, features, :], SL[...], preferred_element_type=jnp.float32)
        G[0, block] = product[:, :COLS].reshape(NX, 64, COLS)
        G[1, block] = product[:, COLS:].reshape(NX, 64, COLS)

    def at_of(part, axis, half, pos, sub=None):
        if part == "A":
            if axis == "x":
                return (0, half * NY + y, pos)
            return (0, half * NY + pos, pl.ds(2 * sub, 2))
        if axis == "x":
            return (1, pl.ds(half * NY + 4 * sub, 4), pos)
        return (1, half * NY + pos, x)

    def room(buf, part, axis, sid):
        return buf[part, axis].at[sid - PLAN["rs", part, axis, 0, 0, 1]]

    def sum_send(part, axis, sub, half, sign, steps, step):
        sid = PLAN["rs", part, axis, sub, half, sign] + step - 1
        own = G[at_of(part, axis, half, place(axis, sign * (steps + 1 - step)), sub)]
        if step > 1:
            own += room(LAND, part, axis, sid - 1)[...].astype(jnp.float32)
        stage = room(STAGE, part, axis, sid)
        stage[...] = own.astype(jnp.bfloat16)
        send(stage, room(LAND, part, axis, sid), sid, ring(axis, sign))

    def sum_step(part, axis, step, sub, only=None):
        for half, sign, steps in chains(NX if axis == "x" else NY):
            if step > steps or (only is not None and steps != only):
                continue
            sid = PLAN["rs", part, axis, sub, half, sign] + step - 1
            arrived(room(LAND, part, axis, sid), sid)
            if step == steps:
                mine_at = at_of(part, axis, half, place(axis, 0), sub)
                G[mine_at] = G[mine_at] + room(LAND, part, axis, sid)[...].astype(jnp.float32)
            else:
                sum_send(part, axis, sub, half, sign, steps, step + 1)

    def direct_send(part, axis):
        size = NX if axis == "x" else NY
        for by in sorted(range(1, size), key=lambda d: -min(d, size - d)):
            for half in range(NZ):
                n = half * (size - 1) + by - 1
                stage = STAGE[part, axis].at[n]
                stage[...] = G[at_of(part, axis, half, place(axis, by))].astype(jnp.bfloat16)
                send(stage, LAND[part, axis].at[n], PLAN["direct", axis] + n, ring(axis, by))

    def direct_take(part, axis, k):
        size = NX if axis == "x" else NY
        for half in range(NZ):
            total = G[at_of(part, axis, half, place(axis, 0))]
            for by in range(1, size):
                n = half * (size - 1) + by - 1
                arrived(LAND[part, axis].at[n], PLAN["direct", axis] + n)
                total += LAND[part, axis][n].astype(jnp.float32)
            FIN[k, half] = total.astype(jnp.bfloat16)

    for half, sign, steps in chains(NY):
        share(half, y + sign * steps)
        sum_send("A", "y", 0, half, sign, steps, 1)
    for half, sign, steps in chains(NY):
        sum_send("A", "y", 1, half, sign, steps, 1)

    def shares(n, carry):
        share(0, y + 3 - n)
        share(1, y - 3 + n)
        return carry

    lax.fori_loop(0, NY - 2, shares, 0)
    for long in (2, 1):
        for sub in range(2):
            for half, sign, steps in chains(NX):
                if steps == long:
                    sum_send("B", "x", sub, half, sign, steps, 1)
    for sub in range(2):
        sum_step("A", "y", 1, sub)
    for sub in range(2):
        sum_step("B", "x", 1, sub, only=2)
    for sub in range(2):
        sum_step("A", "y", 2, sub)
    for sub in range(2):
        sum_step("A", "y", 3, sub)
    for sub in range(2):
        sum_step("B", "x", 1, sub, only=1)
    for sub in range(2):
        sum_step("B", "x", 2, sub)
    direct_send("B", "y")
    for sub in range(2):
        sum_step("A", "y", 4, sub)
    direct_send("A", "x")

    handed = []
    for k, part, axis in ((1, "B", "y"), (0, "A", "x")):
        direct_take(part, axis, k)
        for half in range(NZ):
            for core in range(NC):
                dest_h = k + 2 * zl
                src = FIN.at[k, half, pl.ds(core * 32, 32), :]
                dst = FR.at[h, c]
                rid = PLAN["fn"] + h * NC + c
                sid = PLAN["fn"] + (k * NZ + half) * NC + core
                here = (dest_h == h) & (half == zl) & (core == c)
                remote = pltpu.make_async_remote_copy(
                    src_ref=src,
                    dst_ref=dst,
                    send_sem=ssem.at[sid],
                    recv_sem=rsem.at[rid],
                    device_id=(dest_h, half, y, x, core),
                    device_id_type=MESH,
                )
                keep = pltpu.make_async_copy(src, dst, rsem.at[rid])
                pl.when(here)(keep.start)
                pl.when(jnp.logical_not(here))(remote.start)
                handed.append((here, remote))
    for a in range(NH):
        for core in range(NC):
            arrived(FR.at[a, core], PLAN["fn"] + a * NC + core)
    for core in range(NC):
        parts = [FR[a, core].astype(jnp.float32) for a in range(NH)]
        grad_out[0, :, core * COLS : (core + 1) * COLS] = (parts[0] + parts[1]) + (parts[2] + parts[3])
    for here, remote in handed:
        pl.when(jnp.logical_not(here))(remote.wait_send)
    for when, copy in pend:
        if when is None:
            copy.wait_send()
        else:
            pl.when(when)(copy.wait_send)


def shards(hidden, window_proj, head_weights, ref_logprob, resp_spans):
    vmem = pl.BlockSpec(memory_space=pltpu.VMEM)
    hbm = pl.BlockSpec(memory_space=pl.ANY)
    bf16, f32 = jnp.bfloat16, jnp.float32
    rooms = {
        ("A", "y"): pltpu.VMEM((28, NX // 2, 64, COLS), bf16),
        ("A", "x"): pltpu.VMEM((6, 64, COLS), bf16),
        ("B", "x"): pltpu.VMEM((12, NY // 2, 64, COLS), bf16),
        ("B", "y"): pltpu.VMEM((14, 64, COLS), bf16),
    }
    return pl.pallas_call(
        kernel,
        out_shape=(
            jax.ShapeDtypeStruct((1, 32, 2 * COLS), f32),
            jax.ShapeDtypeStruct((1, LEN), f32),
        ),
        in_specs=[hbm] * 5,
        out_specs=(vmem, vmem),
        scratch_shapes=[
            pltpu.VMEM((NCHIP * NC + 4, TOK, FB), bf16),
            pltpu.VMEM((NH, FB, 4 * COLS), bf16),
            pltpu.VMEM((4, NZ * NY, NX, 64, COLS), bf16),
            pltpu.VMEM((SEQ, 8, COLS), f32),
            pltpu.VMEM((NH, SEQ, 8, COLS), f32),
            pltpu.VMEM((NH, SEQ, 8, COLS), f32),
            pltpu.VMEM((SEQ, TOK, COLS), f32),
            pltpu.VMEM((SEQ, TOK, 4 * COLS), f32),
            pltpu.VMEM((4 * COLS, 2 * COLS), bf16),
            pltpu.VMEM((2, NZ * NY, NX, 64, COLS), f32),
            pltpu.VMEM((3, 8, LEN), f32),
            rooms,
            rooms,
            pltpu.VMEM((2, NZ, 64, COLS), bf16),
            pltpu.VMEM((NH, NC, 32, COLS), bf16),
            pltpu.VMEM((1, LEN), bf16),
            pltpu.VMEM((1, LEN), f32),
            pltpu.SMEM((1, 2), jnp.int32),
            pltpu.SemaphoreType.DMA((PLAN["total"],)),
            pltpu.SemaphoreType.DMA((PLAN["total"],)),
        ],
        compiler_params=pltpu.CompilerParams(
            collective_id=0, has_side_effects=True, vmem_limit_bytes=60 * 1024 * 1024
        ),
    )(hidden, window_proj, head_weights, ref_logprob, resp_spans)


def solution(mesh):
    finer = Mesh(mesh.devices.reshape(NH, NZ, NY, NX, NC), AXES)
    return jax.shard_map(
        shards,
        mesh=finer,
        in_specs=(P(FSDP, "h"), P("h", FSDP, None), P("h", None), P(FSDP, None), P(FSDP, None)),
        out_specs=(P("h", FSDP, None), P(FSDP, None)),
        check_vma=False,
    )
```

```python
import jax
import jax.numpy as jnp
from jax import lax
from jax.experimental import pallas as pl
from jax.experimental.pallas import tpu as pltpu
from jax.sharding import Mesh
from jax.sharding import PartitionSpec as P

AXES = ("h", "zl", "y", "x", "c")
FSDP = AXES[1:]
MESH = pl.DeviceIdType.MESH

NH, NZ, NY, NX, NC = 4, 2, 8, 4, 2
LEN = 512
SKIP = 64
TOK = (LEN - SKIP) // NH
CUT = (48, 64)
SEQ = NZ * NC
ROWS = SEQ * TOK
FB = 1024
COLS = 128
D = NH * FB
NCHIP = NH * NZ

KL_COEF = 0.1
DISCOUNT = 1.0
TRACE_DECAY = 0.95
NORM_EPS = 1e-05
HIGHEST = lax.Precision.HIGHEST

GROUP = [(a, b, e) for a in (2, 1, 3, 0) for b in range(NZ) for e in range(NC) if (a, b, e) != (0, 0, 0)]


def chains(size):
    far, near = size // 2, size // 2 - 1
    return [(0, 1, far), (1, -1, far), (0, -1, near), (1, 1, near)]


def plan():
    out = {}
    used = 0

    def take(name, count):
        nonlocal used
        out[name] = used
        used += count

    for name in ("wg", "sd", "mg"):
        take(name, len(GROUP))
    for odd in range(2):
        for way in (1, -1):
            take(("hn", odd, way), 8)
        take(("hd", odd), 8)
    for part, axis in (("A", "x"), ("B", "y")):
        for half, sign, steps in chains(NX if axis == "x" else NY):
            take(("ag", part, axis, half, sign), steps)
    for sub in range(2):
        for half, sign, steps in chains(NY):
            take(("ag", "A", "y", sub, half, sign), steps)
    for half, sign, steps in chains(NX):
        take(("ag", "B", "x", half, sign), steps * NY)
    for part, axis in (("A", "y"), ("B", "x")):
        for sub in range(2):
            for half, sign, steps in chains(NX if axis == "x" else NY):
                take(("rs", part, axis, sub, half, sign), steps)
    take(("direct", "x"), NZ * (NX - 1))
    take(("direct", "y"), NZ * (NY - 1))
    take("fn", NH * NC)
    take("local", 8)
    out["total"] = used
    return out


PLAN = plan()


def kernel(
    hid, win, head_in, refl_in, spans_in, grad_out, adv_out,
    X, XT, W, SAY, SIDE, MSG, SS, ACC, SL, G, ROWS4, STAGE, LAND, FIN, FR, HEAD, REFL, SPANS,
    ssem, rsem,
):
    h, zl, y, x, c = (lax.axis_index(a) for a in AXES)
    p = zl * NC + c
    pend = []

    def send(src, dst, sid, dev, rid=None, when=None):
        copy = pltpu.make_async_remote_copy(
            src_ref=src,
            dst_ref=dst,
            send_sem=ssem.at[sid],
            recv_sem=rsem.at[sid if rid is None else rid],
            device_id=dev,
            device_id_type=MESH,
        )
        if when is None:
            copy.start()
        else:
            pl.when(when)(copy.start)
        pend.append((when, copy))

    def arrived(ref, sid, when=None):
        copy = pltpu.make_async_copy(ref, ref, rsem.at[sid])
        if when is None:
            copy.wait()
        else:
            pl.when(when)(copy.wait)

    def peer(dh, dz, dc):
        return (lax.rem(h + dh, NH), lax.rem(zl + dz, NZ), y, x, lax.rem(c + dc, NC))

    def origin(dh, dz, dc):
        return (lax.rem(h + NH - dh, NH), lax.rem(zl + NZ - dz, NZ), lax.rem(c + NC - dc, NC))

    def place(axis, by):
        return lax.rem(x + 2 * NX + by, NX) if axis == "x" else lax.rem(y + 2 * NY + by, NY)

    def ring(axis, by):
        if axis == "x":
            return (h, zl, y, place("x", by), c)
        return (h, zl, place("y", by), x, c)

    barrier = pltpu.get_barrier_semaphore()
    mates = [peer(*o) for o in GROUP]
    mates += [ring("x", by) for by in range(1, NX)] + [ring("y", by) for by in range(1, NY)]
    for dev in mates:
        pl.semaphore_signal(barrier, inc=1, device_id=dev, device_id_type=MESH)
    local = PLAN["local"]
    fetches = [
        pltpu.make_async_copy(src, dst, rsem.at[local + n])
        for n, (src, dst) in enumerate(((head_in, HEAD), (refl_in, REFL), (spans_in, SPANS)))
    ]
    for fetch in fetches:
        fetch.start()
    pl.semaphore_wait(barrier, len(mates))

    def wpiece(hs, zs, cs):
        return W.at[hs, zs * NY + y, x, pl.ds(pl.multiple_of(cs * 32, 32), 32), :]

    def wcols(zs, cs):
        return win.at[0, :, pl.ds(pl.multiple_of((zs * NC + cs) * COLS, COLS), COLS)]

    own_w = pltpu.make_async_copy(wcols(zl, c), wpiece(h, zl, c), rsem.at[local + 3])
    own_w.start()
    for n, off in enumerate(GROUP):
        dev = peer(*off)
        send(wcols(dev[1], dev[4]), wpiece(h, zl, c), PLAN["wg"] + n, dev)

    chip = h * NZ + zl
    sibling = (h, zl, y, x, 1 - c)

    def turn(by):
        return lax.rem(chip + 2 * NCHIP + by, NCHIP)

    def next_chip(way):
        to = turn(way)
        return (lax.div(to, NZ), lax.rem(to, NZ), y, x, c)

    def rows_of(odd):
        return pl.ds(0, CUT[0]) if odd == 0 else pl.ds(CUT[0], CUT[1])

    def unit(odd, pair):
        start = SKIP + pair * TOK + (CUT[0] if odd else 0)
        return hid.at[pl.ds(pl.multiple_of(start, 16), CUT[odd]), :]

    def kept(odd, origin, core):
        return X.at[origin * NC + core, rows_of(odd)]

    def passing(odd, way, n):
        return X.at[NCHIP * NC + (0 if way == 1 else 2) + n, rows_of(odd)]

    def side_of(odd, way):
        side = lax.rem(chip + odd, NZ)
        return side if way == 1 else 1 - side

    def hid_sem(odd, way, step, high):
        return PLAN["hn", odd, way] + 2 * (step - 1) + high

    def own_pair(odd):
        return lax.div(turn(-odd), NZ)

    def far_unit(odd, way, high):
        side = side_of(odd, way)
        if way == 1:
            return unit(odd, lax.div(turn(side + 2 * high - odd), NZ))
        return unit(odd, lax.div(turn(-1 - side - 2 * high - odd), NZ))

    def hid_send(odd, way, step, high):
        side = side_of(odd, way)
        origin = turn(-way * (step - 1))
        at_next = kept(odd, origin, c)
        when = None
        if step == 1:
            src = far_unit(odd, way, high)
            dst = passing(odd, way, 0) if high else at_next
        elif step == 2:
            src = passing(odd, way, 0) if high else kept(odd, origin, c)
            dst = at_next
            if high:
                dst = X.at[
                    jnp.where(side == 0, NCHIP * NC + (0 if way == 1 else 2) + 1, origin * NC + c), rows_of(odd)
                ]
            else:
                when = side == 0
        elif step == 3:
            src = X.at[jnp.where(side == 1, NCHIP * NC + (0 if way == 1 else 2) + 1, origin * NC + c), rows_of(odd)]
            dst = at_next
        else:
            src, dst, when = kept(odd, origin, c), at_next, side == 0
        send(src, dst, hid_sem(odd, way, step, high), next_chip(way), when=when)

    def share_unit(odd, n, origin):
        ref = kept(odd, origin, c)
        send(ref, ref, PLAN["hd", odd] + n, sibling)

    ORIGINS = (0, -1, 1, -2, 2, -3, 3, 4)

    def hid_take(odd, way, step, high):
        side = side_of(odd, way)
        origin = turn(-way * step)
        sem = hid_sem(odd, way, step, high)
        n = ORIGINS.index(-way * step) if step < 4 else 7
        ref = kept(odd, origin, c)
        if step == 1 and high:
            arrived(passing(odd, way, 0), sem)
            hid_send(odd, way, 2, 1)
        elif step == 1:
            arrived(ref, sem)
            hid_send(odd, way, 2, 0)
            share_unit(odd, n, origin)
        elif step == 2 and high:
            arrived(ref, sem)
            hid_send(odd, way, 3, 1)
        elif step == 2:
            arrived(ref, sem, side == 1)
            share_unit(odd, n, origin)
        elif step == 3:
            arrived(ref, sem)
            hid_send(odd, way, 4, 1)
            share_unit(odd, n, origin)
        else:
            arrived(ref, sem, side == 1)

    def takes(step, high):
        for odd in (1, 0):
            for way in (1, -1):
                hid_take(odd, way, step, high)
        if step == 4:
            for odd in (1, 0):
                share_unit(odd, 7, turn(4))

    own_x = []
    for odd in range(2):
        keep = pltpu.make_async_copy(unit(odd, own_pair(odd)), kept(odd, chip, c), rsem.at[local + 4 + odd])
        keep.start()
        own_x.append(keep)
    for high in (1, 0):
        for odd in (1, 0):
            for way in (1, -1):
                hid_send(odd, way, 1, high)
    for odd in range(2):
        send(unit(odd, own_pair(odd)), kept(odd, chip, c), PLAN["hd", odd], sibling)

    MSG[h, p] = jnp.zeros((8, COLS), jnp.float32)
    SS[...] = jnp.zeros_like(SS)
    ACC[...] = jnp.zeros_like(ACC)
    SL[...] = jnp.zeros_like(SL)
    for fetch in fetches:
        fetch.wait()
    heads_wide = HEAD[...].astype(jnp.float32)
    for target in range(SEQ):
        for k in range(4):
            SAY[target, k : k + 1, :] = REFL[0:1, k * COLS : (k + 1) * COLS]
        for k in range(2):
            SAY[target, 4 + k : 5 + k, :] = jnp.full((1, COLS), SPANS[0, k], jnp.int32).astype(jnp.float32)
        SAY[target, 6:7, :] = heads_wide[:, target * COLS : (target + 1) * COLS]
        SAY[target, 7:8, :] = jnp.zeros((1, COLS), jnp.float32)
    SIDE[h, p] = SAY[p]
    for n, off in enumerate(GROUP):
        dev = peer(*off)
        send(SAY.at[dev[1] * NC + dev[4]], SIDE.at[h, p], PLAN["sd"] + n, dev)

    def settle(odd, which):
        for n in which:
            if n == 0:
                own_x[odd].wait()
            origin = turn(ORIGINS[n])
            block, low = lax.div(origin, NZ), lax.rem(origin, NZ)
            arrived(kept(odd, origin, 1 - c), PLAN["hd", odd] + n)
            first = 0 if odd == 0 else CUT[0]
            both = X[pl.ds(origin * NC, NC), first : first + CUT[odd], :]
            wide = both.astype(jnp.float32)
            wide = wide * wide
            part = wide[:, :, :COLS]
            for k in range(1, FB // COLS):
                part += wide[:, :, k * COLS : (k + 1) * COLS]
            SS[pl.ds(low * NC, NC), first : first + CUT[odd], :] += part
            flat = both.reshape(NC * CUT[odd], FB)
            if NC * CUT[odd] < COLS:
                flat = jnp.concatenate([flat, jnp.zeros((COLS - NC * CUT[odd], FB), jnp.bfloat16)], axis=0)
            lanes = pl.ds(pl.multiple_of((odd * NZ + low) * COLS, COLS), COLS)
            XT[block, :, lanes] = flat.T

    def piece(part, axis, half, pos):
        if part == "A":
            slabs = pl.ds(0, 2 - half)
        else:
            slabs = pl.ds(2 - half, 2 + half)
        if part == "A":
            if axis == "x":
                return W.at[slabs, half * NY + y, pos]
            return W.at[slabs, half * NY + pos]
        if axis == "y":
            return W.at[slabs, half * NY + pos, x]
        return W.at[slabs, pl.ds(half * NY, NY), pos]

    def gather_start(part, axis):
        for half, sign, _ in chains(NX if axis == "x" else NY):
            own = piece(part, axis, half, place(axis, 0))
            send(own, own, PLAN["ag", part, axis, half, sign], ring(axis, sign))

    def gather_step(part, axis, step):
        for half, sign, steps in chains(NX if axis == "x" else NY):
            if step > steps:
                continue
            base = PLAN["ag", part, axis, half, sign]
            got = piece(part, axis, half, place(axis, -sign * step))
            arrived(got, base + step - 1)
            if step < steps:
                send(got, got, base + step, ring(axis, sign))
            if part == "B":
                across_start(half, (-sign * step) % NY)

    def along(half, by, sub):
        return W.at[pl.ds(0, 2 - half), half * NY + place("y", by), pl.ds(2 * sub, 2)]

    def along_start(sub):
        for half, sign, _ in chains(NY):
            own = along(half, 0, sub)
            send(own, own, PLAN["ag", "A", "y", sub, half, sign], ring("y", sign))

    def along_step(step):
        for sub in range(2):
            for half, sign, steps in chains(NY):
                if step > steps:
                    continue
                base = PLAN["ag", "A", "y", sub, half, sign]
                got = along(half, -sign * step, sub)
                arrived(got, base + step - 1)
                if step < steps:
                    send(got, got, base + step, ring("y", sign))

    def cell(half, by, pos):
        return W.at[pl.ds(2 - half, 2 + half), half * NY + place("y", by), pos]

    def across_start(half, by):
        for other, sign, steps in chains(NX):
            if other == half:
                own = cell(half, by, x)
                send(own, own, PLAN["ag", "B", "x", half, sign] + by * steps, ring("x", sign))

    def across_step(by, step):
        for half, sign, steps in chains(NX):
            if step > steps:
                continue
            base = PLAN["ag", "B", "x", half, sign] + by * steps
            got = cell(half, by, place("x", -sign * step))
            arrived(got, base + step - 1)
            if step < steps:
                send(got, got, base + step, ring("x", sign))

    own_w.wait()
    for n, off in enumerate(GROUP):
        arrived(wpiece(*origin(*off)), PLAN["wg"] + n)
    gather_start("A", "x")
    gather_start("B", "y")
    for half in range(NZ):
        across_start(half, 0)
    takes(1, 1)
    gather_step("A", "x", 1)
    gather_step("B", "y", 1)
    gather_step("A", "x", 2)
    for sub in range(2):
        along_start(sub)
    across_step(0, 1)
    gather_step("B", "y", 2)
    gather_step("B", "y", 3)
    takes(1, 0)
    across_step(1, 1)
    across_step(7, 1)
    gather_step("B", "y", 4)
    takes(2, 1)
    along_step(1)
    across_step(2, 1)
    across_step(6, 1)
    takes(2, 0)
    along_step(2)
    across_step(3, 1)
    across_step(5, 1)
    takes(3, 1)
    across_step(4, 1)
    along_step(3)
    takes(4, 1)
    for odd in range(2):
        settle(odd, (0, 1, 2,))
    for odd in range(2):
        settle(odd, (3, 4,))
    for odd in range(2):
        settle(odd, (5, 6, 7,))
    along_step(4)

    def project(j, k):
        tokens = X[pl.ds(4 * j, 4)].reshape(ROWS, FB)
        sides = [W[2 * k + e, pl.ds(4 * j, 4)].reshape(FB, COLS) for e in range(2)]
        both = jnp.concatenate(sides, axis=1)
        product = jnp.dot(tokens, both, preferred_element_type=jnp.float32)
        ACC[:, :, 2 * COLS * k : 2 * COLS * (k + 1)] += product.reshape(SEQ, TOK, 2 * COLS)
        return 0

    lax.fori_loop(0, NH // 2, lambda j, carry: project(j, 0), 0)
    for by in range(NY):
        across_step(by, 2)
    for n, off in enumerate(GROUP):
        hs, zs, cs = origin(*off)
        arrived(SIDE.at[hs, zs * NC + cs], PLAN["sd"] + n)

    lax.fori_loop(NH // 2, NH, lambda j, carry: project(j, 0), 0)
    lax.fori_loop(0, NH, lambda j, carry: project(j, 1), 0)

    heads = [SIDE[s, p, 6:7, :] for s in range(4)]
    ones = jnp.ones((8, COLS), jnp.float32)

    def row_sums(values):
        sums = lax.dot_general(
            ones, values, (((1,), (1,)), ((), ())), precision=HIGHEST, preferred_element_type=jnp.float32
        )
        return sums[0:1, :]

    lane = lax.broadcasted_iota(jnp.int32, (1, COLS), 1)
    blocks = (h, lax.rem(h + 3 + zl, NH))
    at_lane = (lane + SKIP + TOK * jnp.where(lane < CUT[0], blocks[0], blocks[1])).astype(jnp.float32)[:, :TOK]
    for i in range(SEQ):
        starts, ending = SIDE[h, i, 4:5, 0:TOK], SIDE[h, i, 5:6, 0:TOK]
        inside = jnp.where((at_lane >= starts) & (at_lane < ending), 1.0, 0.0)
        last_tok = jnp.where(at_lane == ending - 1.0, 1.0, 0.0)
        meansq = jnp.sum(SS[i], axis=1, keepdims=True) * (1.0 / D)
        scale = lax.rsqrt(meansq + NORM_EPS)
        weighted = []
        for s in range(4):
            raw = ACC[i, :, s * COLS : (s + 1) * COLS] * scale
            pre = raw.astype(jnp.bfloat16).astype(jnp.float32)
            sigmoid = 1.0 / (1.0 + jnp.exp(-pre))
            weighted.append(heads[s] * (pre * sigmoid))
            if s < 2:
                slope = sigmoid * (1.0 + pre * (1.0 - sigmoid))
                ACC[i, :, s * COLS : (s + 1) * COLS] = scale * heads[s] * slope
        log_prob = row_sums(weighted[0] + weighted[1])
        MSG[h, p, i : i + 1, 0:TOK] = -KL_COEF * log_prob * inside + row_sums(weighted[3]) * last_tok
        MSG[h, p, 4 + i : 5 + i, 0:TOK] = row_sums(weighted[2])
    for n, off in enumerate(GROUP):
        send(MSG.at[h, p], MSG.at[h, p], PLAN["mg"] + n, peer(*off))

    for i in range(SEQ):
        for k in range(4):
            part = slice(k * COLS, (k + 1) * COLS)
            ROWS4[0, i : i + 1, part] = SIDE[h, i, k : k + 1, :]
            ROWS4[1, i : i + 1, part] = SIDE[h, i, 4:5, :]
            ROWS4[2, i : i + 1, part] = SIDE[h, i, 5:6, :]
    for n, off in enumerate(GROUP):
        hs, zs, cs = origin(*off)
        arrived(MSG.at[hs, zs * NC + cs], PLAN["mg"] + n)

    whole = jnp.zeros((8, LEN), jnp.float32)
    for a in range(NH):
        nxt = (a + 1) % NH
        early = jnp.where(lane < CUT[0], MSG[a, 0] + MSG[a, 1], MSG[nxt, 0] + MSG[nxt, 1])
        total = early + (MSG[a, 2] + MSG[a, 3])
        wide = jnp.concatenate([total, jnp.zeros((8, LEN - COLS), jnp.float32)], axis=1)
        whole += pltpu.roll(wide, SKIP + a * TOK, 1)
    gains, value_est = whole[0:4], whole[4:8]
    position = lax.broadcasted_iota(jnp.int32, (SEQ, LEN), 1)
    ref, starts, ending = ROWS4[0, 0:4, :], ROWS4[1, 0:4, :], ROWS4[2, 0:4, :]
    at = position.astype(jnp.float32)
    inside = jnp.where((at >= starts) & (at < ending), 1.0, 0.0)
    follow = jnp.where(at + 1.0 < ending, 1.0, 0.0)
    reward = gains + KL_COEF * ref * inside
    next_value = pltpu.roll(value_est, LEN - 1, 1)
    trail = (reward + DISCOUNT * next_value * follow - value_est) * inside
    span = 1
    while span < LEN:
        later = jnp.where(position + span < LEN, pltpu.roll(trail, LEN - span, 1), 0.0)
        trail += (DISCOUNT * TRACE_DECAY) ** span * later
        span *= 2
    advantage = trail * inside
    signal = -advantage / (ending - starts)
    mine = lax.broadcasted_iota(jnp.int32, (SEQ, LEN), 0) == p
    adv_out[...] = jnp.sum(jnp.where(mine, advantage, 0.0), axis=0, keepdims=True)

    near = jnp.zeros((SEQ, COLS), jnp.float32)
    for a in range(NH):
        turned = pltpu.roll(signal, LEN - SKIP - a * TOK, 1)[:, :COLS]
        wanted = jnp.where(lane < CUT[0], blocks[0], blocks[1]) == a
        near += jnp.where(wanted, turned, 0.0)
    square = jnp.concatenate([near, jnp.zeros((COLS - SEQ, COLS), jnp.float32)], axis=0).T
    for i in range(SEQ):
        factor = square[0:TOK, i : i + 1]
        slopes = (factor * ACC[i, :, 0 : 2 * COLS]).astype(jnp.bfloat16)
        low, core = i // NC, i % NC
        for odd in range(2):
            first = (odd * NZ + low) * COLS + core * CUT[odd]
            taken = slice(0, CUT[0]) if odd == 0 else slice(CUT[0], TOK)
            SL[first : first + CUT[odd], :] = slopes[taken]

    def share(half, pos):
        block = half * NY + lax.rem(pos + 2 * NY, NY)
        j = lax.div(block, 4)
        features = pl.ds(pl.multiple_of(lax.rem(block, 4) * 256, 256), 256)
        product = jnp.dot(XT[j, features, :], SL[...], preferred_element_type=jnp.float32)
        G[0, block] = product[:, :COLS].reshape(NX, 64, COLS)
        G[1, block] = product[:, COLS:].reshape(NX, 64, COLS)

    def at_of(part, axis, half, pos, sub=None):
        if part == "A":
            if axis == "x":
                return (0, half * NY + y, pos)
            return (0, half * NY + pos, pl.ds(2 * sub, 2))
        if axis == "x":
            return (1, pl.ds(half * NY + 4 * sub, 4), pos)
        return (1, half * NY + pos, x)

    def room(buf, part, axis, sid):
        return buf[part, axis].at[sid - PLAN["rs", part, axis, 0, 0, 1]]

    def sum_send(part, axis, sub, half, sign, steps, step):
        sid = PLAN["rs", part, axis, sub, half, sign] + step - 1
        own = G[at_of(part, axis, half, place(axis, sign * (steps + 1 - step)), sub)]
        if step > 1:
            own += room(LAND, part, axis, sid - 1)[...].astype(jnp.float32)
        stage = room(STAGE, part, axis, sid)
        stage[...] = own.astype(jnp.bfloat16)
        send(stage, room(LAND, part, axis, sid), sid, ring(axis, sign))

    def sum_step(part, axis, step, sub, only=None):
        for half, sign, steps in chains(NX if axis == "x" else NY):
            if step > steps or (only is not None and steps != only):
                continue
            sid = PLAN["rs", part, axis, sub, half, sign] + step - 1
            arrived(room(LAND, part, axis, sid), sid)
            if step == steps:
                mine_at = at_of(part, axis, half, place(axis, 0), sub)
                G[mine_at] = G[mine_at] + room(LAND, part, axis, sid)[...].astype(jnp.float32)
            else:
                sum_send(part, axis, sub, half, sign, steps, step + 1)

    def direct_send(part, axis):
        size = NX if axis == "x" else NY
        for by in sorted(range(1, size), key=lambda d: -min(d, size - d)):
            for half in range(NZ):
                n = half * (size - 1) + by - 1
                stage = STAGE[part, axis].at[n]
                stage[...] = G[at_of(part, axis, half, place(axis, by))].astype(jnp.bfloat16)
                send(stage, LAND[part, axis].at[n], PLAN["direct", axis] + n, ring(axis, by))

    def direct_take(part, axis, k):
        size = NX if axis == "x" else NY
        for half in range(NZ):
            total = G[at_of(part, axis, half, place(axis, 0))]
            for by in range(1, size):
                n = half * (size - 1) + by - 1
                arrived(LAND[part, axis].at[n], PLAN["direct", axis] + n)
                total += LAND[part, axis][n].astype(jnp.float32)
            FIN[k, half] = total.astype(jnp.bfloat16)

    for half, sign, steps in chains(NY):
        share(half, y + sign * steps)
        sum_send("A", "y", 0, half, sign, steps, 1)
    for half, sign, steps in chains(NY):
        sum_send("A", "y", 1, half, sign, steps, 1)

    def shares(n, carry):
        share(0, y + 3 - n)
        share(1, y - 3 + n)
        return carry

    lax.fori_loop(0, NY - 2, shares, 0)
    for long in (2, 1):
        for sub in range(2):
            for half, sign, steps in chains(NX):
                if steps == long:
                    sum_send("B", "x", sub, half, sign, steps, 1)
    for sub in range(2):
        sum_step("A", "y", 1, sub)
    for sub in range(2):
        sum_step("B", "x", 1, sub, only=2)
    for sub in range(2):
        sum_step("A", "y", 2, sub)
    for sub in range(2):
        sum_step("A", "y", 3, sub)
    for sub in range(2):
        sum_step("B", "x", 1, sub, only=1)
    for sub in range(2):
        sum_step("B", "x", 2, sub)
    direct_send("B", "y")
    for sub in range(2):
        sum_step("A", "y", 4, sub)
    direct_send("A", "x")

    handed = []
    for k, part, axis in ((1, "B", "y"), (0, "A", "x")):
        direct_take(part, axis, k)
        for half in range(NZ):
            for core in range(NC):
                dest_h = k + 2 * zl
                src = FIN.at[k, half, pl.ds(core * 32, 32), :]
                dst = FR.at[h, c]
                rid = PLAN["fn"] + h * NC + c
                sid = PLAN["fn"] + (k * NZ + half) * NC + core
                here = (dest_h == h) & (half == zl) & (core == c)
                remote = pltpu.make_async_remote_copy(
                    src_ref=src,
                    dst_ref=dst,
                    send_sem=ssem.at[sid],
                    recv_sem=rsem.at[rid],
                    device_id=(dest_h, half, y, x, core),
                    device_id_type=MESH,
                )
                keep = pltpu.make_async_copy(src, dst, rsem.at[rid])
                pl.when(here)(keep.start)
                pl.when(jnp.logical_not(here))(remote.start)
                handed.append((here, remote))
    for a in range(NH):
        for core in range(NC):
            arrived(FR.at[a, core], PLAN["fn"] + a * NC + core)
    for core in range(NC):
        parts = [FR[a, core].astype(jnp.float32) for a in range(NH)]
        grad_out[0, :, core * COLS : (core + 1) * COLS] = (parts[0] + parts[1]) + (parts[2] + parts[3])
    for here, remote in handed:
        pl.when(jnp.logical_not(here))(remote.wait_send)
    for when, copy in pend:
        if when is None:
            copy.wait_send()
        else:
            pl.when(when)(copy.wait_send)


def shards(hidden, window_proj, head_weights, ref_logprob, resp_spans):
    vmem = pl.BlockSpec(memory_space=pltpu.VMEM)
    hbm = pl.BlockSpec(memory_space=pl.ANY)
    bf16, f32 = jnp.bfloat16, jnp.float32
    rooms = {
        ("A", "y"): pltpu.VMEM((28, NX // 2, 64, COLS), bf16),
        ("A", "x"): pltpu.VMEM((6, 64, COLS), bf16),
        ("B", "x"): pltpu.VMEM((12, NY // 2, 64, COLS), bf16),
        ("B", "y"): pltpu.VMEM((14, 64, COLS), bf16),
    }
    return pl.pallas_call(
        kernel,
        out_shape=(
            jax.ShapeDtypeStruct((1, 32, 2 * COLS), f32),
            jax.ShapeDtypeStruct((1, LEN), f32),
        ),
        in_specs=[hbm] * 5,
        out_specs=(vmem, vmem),
        scratch_shapes=[
            pltpu.VMEM((NCHIP * NC + 4, TOK, FB), bf16),
            pltpu.VMEM((NH, FB, 4 * COLS), bf16),
            pltpu.VMEM((4, NZ * NY, NX, 64, COLS), bf16),
            pltpu.VMEM((SEQ, 8, COLS), f32),
            pltpu.VMEM((NH, SEQ, 8, COLS), f32),
            pltpu.VMEM((NH, SEQ, 8, COLS), f32),
            pltpu.VMEM((SEQ, TOK, COLS), f32),
            pltpu.VMEM((SEQ, TOK, 4 * COLS), f32),
            pltpu.VMEM((4 * COLS, 2 * COLS), bf16),
            pltpu.VMEM((2, NZ * NY, NX, 64, COLS), f32),
            pltpu.VMEM((3, 8, LEN), f32),
            rooms,
            rooms,
            pltpu.VMEM((2, NZ, 64, COLS), bf16),
            pltpu.VMEM((NH, NC, 32, COLS), bf16),
            pltpu.VMEM((1, LEN), bf16),
            pltpu.VMEM((1, LEN), f32),
            pltpu.SMEM((1, 2), jnp.int32),
            pltpu.SemaphoreType.DMA((PLAN["total"],)),
            pltpu.SemaphoreType.DMA((PLAN["total"],)),
        ],
        compiler_params=pltpu.CompilerParams(
            collective_id=0, has_side_effects=True, vmem_limit_bytes=60 * 1024 * 1024
        ),
    )(hidden, window_proj, head_weights, ref_logprob, resp_spans)


def solution(mesh):
    finer = Mesh(mesh.devices.reshape(NH, NZ, NY, NX, NC), AXES)
    return jax.shard_map(
        shards,
        mesh=finer,
        in_specs=(P(FSDP, "h"), P("h", FSDP, None), P("h", None), P(FSDP, None), P(FSDP, None)),
        out_specs=(P("h", FSDP, None), P(FSDP, None)),
        check_vma=False,
    )
```
